256 devices in a mesh: leaf: 256 (over z, y, x, core).
Axes of the slice: x: 4, y: 4, z: 8, core: 2. Of those that a mesh axis runs over, the one named last changes fastest.
Arguments:
- loads: bfloat16 [524288, 128], P('leaf'), may hold values from -6 to 6
- leaf_inverse: bfloat16 [524288, 2048], P('leaf'), may hold values from -0.125 to 0.125
- bases: bfloat16 [5, 524288, 128], P(None, 'leaf'), may hold values from -0.375 to 0.375
- couplings: bfloat16 [5, 256, 256, 256], P(None, 'leaf'), as said below
Outputs:
- solution: float32 [524288, 128], P('leaf')
The draws below stay inside these ranges and needn't reach their ends.
Inputs may be any that keep to these rules, and one draw needn't show every extreme that they name: couplings[l, d] is the same matrix for all leaves d of one level-l node, that is for each run of 256 / 2**l consecutive leaves.
All inputs are finite; a program needn't handle non-finite values.
Results may differ from the reference program's by a relative error of at most 0.018.
Values sent between devices are 32-bit elements; how exact they have to be, the bound alone decides.
A program may use at most 64 MiB of HBM per device.

```python
import math
import jax
import jax.numpy as jnp
from jax import lax

LEAF = 2048
RANK = 128
CASES = 128
LEVELS = 5
NLEAVES = 256
ORDER = 524288


def draw_couplings(key, part):
    key = jax.random.fold_in(key, 7)
    layers = []
    for level_no in range(LEVELS):
        nodes = 2 ** level_no
        group_size = NLEAVES // nodes
        child_rows = LEAF * group_size // 2
        factor = 1.0 / math.sqrt(child_rows)
        sub_key = jax.random.fold_in(key, level_no)
        base = jax.random.normal(sub_key, (nodes, 2 * RANK, 2 * RANK), jnp.float32)
        layers.append(jnp.repeat(base * factor, group_size, axis=0))
    return jnp.stack(layers).astype(jnp.bfloat16)


def block_scale(key, dims, split, low, high):
    level, own = 1.0, jax.random.fold_in(key, 6)
    for dim, parts in split:
        heights = jnp.exp(jax.random.uniform(jax.random.fold_in(own, dim), (parts,), jnp.float32, low / len(split), high / len(split)))
        level = level * jnp.repeat(heights, dims[dim] // parts).reshape([-1 if axis == dim else 1 for axis in range(len(dims))])
    return level


def noise(key, extent, spread, reach, shards=(), kind=jnp.bfloat16):
    factor_of = block_scale(key, extent, shards, -0.22, 0.18) if shards else 1.0
    values = jax.random.normal(key, extent, jnp.float32) * spread * factor_of
    return jnp.minimum(jnp.maximum(values, -reach), reach).astype(kind)


def setup_inputs(seed: int = 0) -> dict:
    splits = jax.random.split(jax.random.key(seed), 5)
    return {
        "loads": noise(splits[0], (ORDER, CASES), 1.0, 6.0, ((0, 256),)),
        "leaf_inverse": noise(splits[1], (ORDER, LEAF), LEAF ** -0.5, 0.125, ((0, 256),)),
        "bases": noise(splits[2], (LEVELS, ORDER, RANK), 0.0625, 0.375, ((1, 256),)),
        "couplings": draw_couplings(jax.random.fold_in(splits[4], 71), 0),
    }


def leaf_product(pair):
    return jnp.dot(pair[0], pair[1], preferred_element_type=jnp.float32)


def reference(loads, leaf_inverse, bases, couplings):
    blocks = leaf_inverse.reshape(NLEAVES, LEAF, LEAF)
    sides = loads.reshape(NLEAVES, LEAF, CASES)
    field = lax.map(leaf_product, (blocks, sides)).reshape(ORDER, CASES)
    for sweep_turn in range(LEVELS):
        level_no = LEVELS - 1 - sweep_turn
        nodes = 2 ** level_no
        half_rows = ORDER // (2 * nodes)
        group_size = NLEAVES // nodes
        field_b = lax.optimization_barrier(field.astype(jnp.bfloat16)).astype(jnp.float32)
        basis = bases[level_no].astype(jnp.float32).reshape(nodes, 2, half_rows, RANK)
        shaped = field_b.reshape(nodes, 2, half_rows, CASES)
        projected = jnp.einsum("nchr,nchk->ncrk", basis, shaped, precision=lax.Precision.HIGHEST)
        stacked = projected.reshape(nodes, 2 * RANK, CASES)
        node_caps = couplings[level_no, ::group_size].astype(jnp.float32)
        coeffs = jnp.einsum("nij,njk->nik", node_caps, stacked, precision=lax.Precision.HIGHEST)
        coeffs = coeffs.astype(jnp.bfloat16).astype(jnp.float32).reshape(nodes, 2, RANK, CASES)
        update = jnp.einsum("nchr,ncrk->nchk", basis, coeffs, precision=lax.Precision.HIGHEST)
        field = field - update.reshape(ORDER, CASES)
    return field
```

```python
import jax
import jax.numpy as jnp
from jax import lax
from jax.experimental import pallas as pl
from jax.experimental.pallas import tpu as pltpu
from jax.sharding import PartitionSpec as P

MESH = pl.DeviceIdType.MESH
F32 = jnp.float32
BF16 = jnp.bfloat16
RANK = 128
CASES = 128
LEVELS = 5
QUARTER = CASES // 4
ROWS = 256


def flip(value, bit):
    return value + bit - 2 * bit * ((value // bit) % 2)


def flips(value, mask):
    for bit in (1, 2, 4):
        if mask & bit:
            value = flip(value, bit)
    return value


def dot_tn(a, b):
    return lax.dot_general(a, b, (((0,), (0,)), ((), ())), preferred_element_type=F32)


def dot_nt(a, b):
    return lax.dot_general(a, b, (((1,), (1,)), ((), ())), preferred_element_type=F32)


def two_parts(value):
    high = value.astype(BF16)
    return high, (value - high.astype(F32)).astype(BF16)


def times_gram(z, gram):
    high, low = two_parts(gram)
    return jnp.dot(
        jnp.concatenate([z, z], 1), jnp.concatenate([high, low], 0), preferred_element_type=F32
    )


GROUPS = (((4, 3),), ((4, 2), (3, 2)), ((4, 0), (4, 1), (3, 0), (3, 1)), ((2, 0), (2, 1), (1, 0)))


def tree_kernel(
    loads_hbm, inverse_hbm, bases_hbm, caps_hbm,
    part_hbm, z0_out,
    loads, inverse, bcat, caps, field, pacc,
    sa, sb, sc, sd, sa_in, sb_in, sc_in, sd_in, sa_rs, sb_rs, sc_rs, sd_rs,
    sa_own, sb_own, sc_own, sd_own, sd_y, gd_own, se_own, se_z, ge_own,
    ga, gb, gc, gd, ge,
    p4, p3, pr, p4_in, p3_in, pr_in, p4_rs, p3_rs, pr_rs,
    e3, l3, e2, l2, e10, l2r, e1, l1, f0, l1r, e0, l0,
    zown, zbuf,
    local_sem, chunk_sem, out_sem, send_sem, recv_sem,
):
    rows = field.shape[0]
    steps = rows // ROWS
    me = lax.axis_index("leaf")
    core = me % 2
    x = (me // 2) % 4
    y = (me // 8) % 4
    z = me // 32

    def device(dx=0, dy=0, dz=0, on=1):
        return ((flips(z, dz) * 4 + flips(y, dy)) * 4 + flips(x, dx)) * 2 + on

    loads_in = []
    for level in range(LEVELS):
        copy = pltpu.make_async_copy(
            bases_hbm.at[level], bcat.at[:, pl.ds(level * RANK, RANK)], local_sem.at[level]
        )
        copy.start()
        loads_in.append(copy)
    loads_copy = pltpu.make_async_copy(loads_hbm, loads, local_sem.at[LEVELS])
    loads_copy.start()
    caps_copy = pltpu.make_async_copy(caps_hbm, caps, local_sem.at[LEVELS + 1])

    def inverse_copy(step):
        part = pl.ds(pl.multiple_of(step * ROWS, ROWS), ROWS)
        return pltpu.make_async_copy(inverse_hbm.at[part], inverse.at[part], chunk_sem.at[step])

    for step in range(steps):
        inverse_copy(step).start()
    caps_copy.start()

    barrier = pltpu.get_barrier_semaphore()

    def greet(partners):
        for partner in partners:
            pl.semaphore_signal(barrier, inc=1, device_id=(partner,), device_id_type=MESH)

    gram_partners = (
        [device(dx=j, on=0) for j in (1, 2, 3)]
        + [device(dy=j, on=0) for j in (1, 2, 3)]
        + [device(dz=1, on=0)]
        + [device(dx=j, on=1) for j in range(4)]
    )
    chain_partners = (
        [device(dx=j, on=0) for j in range(4)]
        + [device(dx=j) for j in (1, 2, 3)]
        + [device(dx=j, dy=1) for j in range(4)]
        + [device(dy=j) for j in (2, 3)]
        + [device(dy=j, dz=1) for j in range(4)]
        + [device(dz=j) for j in (2, 3, 7, 5)]
    )

    @pl.when(core == 0)
    def _():
        greet(gram_partners)

    @pl.when(core == 1)
    def _():
        greet(chain_partners)

    for copy in loads_in:
        copy.wait()
    grams = (sa, sb, sc, sd)
    for ref in grams:
        ref[...] = jnp.zeros_like(ref)

    def gram_step(step, carry):
        part = pl.ds(pl.multiple_of(step * ROWS, ROWS), ROWS)
        for level in (4, 3, 2, 1):
            got = dot_tn(
                bcat[part, level * RANK : (level + 1) * RANK], bcat[part, : level * RANK]
            )
            for ref, group in zip(grams, GROUPS):
                for place, (source, target) in enumerate(group):
                    if source == level:
                        ref[:, place * RANK : (place + 1) * RANK] += got[
                            :, target * RANK : (target + 1) * RANK
                        ]
        return carry

    lax.fori_loop(0, steps, gram_step, 0)

    @pl.when(core == 0)
    def _():
        pl.semaphore_wait(barrier, len(gram_partners))

    @pl.when(core == 1)
    def _():
        pl.semaphore_wait(barrier, len(chain_partners))

    counter = [0]

    def message(src, dst, target):
        number = counter[0]
        counter[0] += 1
        return pltpu.make_async_remote_copy(
            src_ref=src, dst_ref=dst, send_sem=send_sem.at[number], recv_sem=recv_sem.at[number],
            device_id=(target,), device_id_type=MESH,
        )

    def quarter(index):
        return pl.ds(pl.multiple_of(index * QUARTER, QUARTER), QUARTER)

    other = device(on=1 - core)
    grams_in = (sa_in, sb_in, sc_in, sd_in)
    gram_pair = [message(src, dst, other) for src, dst in zip(grams, grams_in)]

    @pl.when(core == 1)
    def _():
        for copy in gram_pair:
            copy.start()

    loads_copy.wait()
    pacc[...] = jnp.zeros_like(pacc)

    def field_step(step, carry):
        inverse_copy(step).wait()
        part = pl.ds(pl.multiple_of(step * ROWS, ROWS), ROWS)
        got = jnp.dot(inverse[part, :], loads[...], preferred_element_type=F32)
        field[part, :] = got
        high, low = two_parts(got)
        pacc[...] += dot_tn(jnp.concatenate([high, low], 1), bcat[part, :])
        return carry

    lax.fori_loop(0, steps // 2, field_step, 0)

    rs_slots = (sa_rs, sb_rs, sc_rs, sd_rs)
    gram_rs = [
        [message(src.at[quarter(flips(x, j))], dst.at[j - 1], device(dx=j, on=0)) for j in (1, 2, 3)]
        for src, dst in zip(grams, rs_slots)
    ]

    def pair_sum(group):
        gram_pair[group].wait_recv()
        grams[group][...] += grams_in[group][...]
        for copy in gram_rs[group]:
            copy.start()

    @pl.when(core == 0)
    def _():
        for group in range(4):
            pair_sum(group)

    lax.fori_loop(steps // 2, steps, field_step, 0)

    ordered = (p4, p3, pr)
    columns = ((4 * RANK, 5 * RANK), (3 * RANK, 4 * RANK), (0, 3 * RANK))
    for ref, (low, high) in zip(ordered, columns):
        ref[...] = pacc[:CASES, low:high] + pacc[CASES:, low:high]

    ordered_in = (p4_in, p3_in, pr_in)
    proj_pair = [message(src, dst, other) for src, dst in zip(ordered, ordered_in)]
    own_q = quarter(x)

    z_targets = [(j, on) for on in (1, 0) for j in range(4) if (j, on) != (0, 1)]
    z_out = [
        [message(zown.at[level], zbuf.at[level, own_q], device(dx=j, on=on)) for j, on in z_targets]
        for level in range(LEVELS)
    ]

    def z_wait(level, on):
        for (j, to), copy in zip(z_targets, z_out[level]):
            if to == on:
                copy.wait_recv()

    def subtract(levels):
        factors = jnp.concatenate([zbuf[level].astype(BF16) for level in levels], 1)
        low, high = levels[0] * RANK, (levels[-1] + 1) * RANK

        def step_(step, carry):
            part = pl.ds(pl.multiple_of(step * ROWS, ROWS), ROWS)
            field[part, :] -= dot_nt(bcat[part, low:high], factors)
            return carry

        lax.fori_loop(0, steps, step_, 0)

    def finish(on):
        out = pltpu.make_async_copy(field, part_hbm, out_sem)
        out.start()
        z_wait(0, on)
        z0_out[...] = zbuf[0].astype(BF16)
        out.wait()

    caps_copy.wait()

    gram_own = (sa_own, sb_own, sc_own, sd_own)
    gram_out = [
        [message(src, dst.at[own_q], device(dx=j)) for j in range(4)]
        for src, dst in ((sa_own, ga), (sb_own, gb), (sc_own, gc), (gd_own, gd), (ge_own, ge))
    ]
    plane_out = [message(sd_own, sd_y.at[j - 1], device(dy=j, on=0)) for j in (1, 2, 3)]
    pair_out = message(se_own, se_z, device(dz=1, on=0))

    def row_sum(group):
        for copy in gram_rs[group]:
            copy.wait_recv()
        slots = rs_slots[group]
        gram_own[group][...] = (
            grams[group][own_q, :] + slots[0] + slots[1] + slots[2]
        )

    def start(copies):
        for copy in copies:
            copy.start()

    def wait_recv(copies):
        for copy in copies:
            copy.wait_recv()

    def wait_send(copies):
        for copy in copies:
            copy.wait_send()

    @pl.when(core == 0)
    def _():
        start(proj_pair)
        for group in (0, 1):
            row_sum(group)
            start(gram_out[group])
        row_sum(3)
        start(plane_out)
        row_sum(2)
        start(gram_out[2])
        wait_recv(plane_out)
        total = sd_own[...] + sd_y[0] + sd_y[1] + sd_y[2]
        gd_own[...] = total[:, : 2 * RANK]
        se_own[...] = total[:, 2 * RANK :]
        pair_out.start()
        start(gram_out[3])
        pair_out.wait_recv()
        ge_own[...] = se_own[...] + se_z[...]
        start(gram_out[4])
        for level in (4, 3, 2, 1):
            z_wait(level, 0)
        subtract((1, 2, 3, 4))
        finish(0)
        for copies in gram_rs + gram_out + [plane_out, [pair_out], proj_pair]:
            wait_send(copies)

    def child_side(level):
        return ((y % 2), (y // 2), (z % 2), (z // 2) % 2, (z // 4))[4 - level]

    def solve(level, own, sibling):
        side = child_side(level)
        first = jnp.where(side == 0, own, sibling)
        second = jnp.where(side == 0, sibling, own)
        high, low = two_parts(jnp.concatenate([first, second], 1))
        half = pl.ds(pl.multiple_of(side * RANK, RANK), RANK)
        got = dot_nt(jnp.concatenate([high, low], 0), caps[level, 0, half, :])
        rounded = (got[:QUARTER] + got[QUARTER:]).astype(BF16)
        zown[level] = rounded.astype(F32)
        zbuf[level, own_q, :] = rounded.astype(F32)
        return rounded

    p4_out = [message(p4.at[quarter(flips(x, j))], p4_rs.at[j], device(dx=j)) for j in (1, 2, 3)] + [
        message(p4.at[quarter(flips(x, j))], p4_rs.at[4 + j], device(dx=j, dy=1)) for j in range(4)
    ]
    p3_out = [message(p3.at[quarter(flips(x, j))], p3_rs.at[j - 1], device(dx=j)) for j in (1, 2, 3)]
    pr_out = [message(pr.at[quarter(flips(x, j))], pr_rs.at[j - 1], device(dx=j)) for j in (1, 2, 3)]
    e3_out = [message(e3, l3.at[j - 1], device(dy=j)) for j in (1, 2, 3)]
    e2_out = [
        message(e2, l2.at[4 * k + j], device(dy=j, dz=k))
        for k in (0, 1) for j in range(4) if (j, k) != (0, 0)
    ]
    e10_out = [message(e10, l2r.at[j - 1], device(dy=j)) for j in (1, 2, 3)]
    e1_out = [message(e1, l1.at[j - 1], device(dz=j)) for j in (1, 2, 3)]
    f0_out = message(f0, l1r, device(dz=1))
    e0_out = [message(e0, l0.at[i], device(dz=j)) for i, j in enumerate((2, 7, 5))]

    def block(ref, place):
        return ref[:, place * RANK : (place + 1) * RANK]

    @pl.when(core == 1)
    def _():
        proj_pair[0].wait_recv()
        p4[...] += p4_in[...]
        start(p4_out)
        proj_pair[1].wait_recv()
        p3[...] += p3_in[...]
        start(p3_out)
        proj_pair[2].wait_recv()
        pr[...] += pr_in[...]
        start(pr_out)

        wait_recv(p4_out)
        own = p4[own_q, :] + p4_rs[1] + p4_rs[2] + p4_rs[3]
        z4 = solve(4, own, p4_rs[4] + p4_rs[5] + p4_rs[6] + p4_rs[7])
        wait_recv(p3_out)
        wait_recv(gram_out[0])
        own = p3[own_q, :] + p3_rs[0] + p3_rs[1] + p3_rs[2] - times_gram(z4, ga[...])
        e3[...] = own
        start(e3_out)
        start(z_out[4])

        wait_recv(pr_out)
        rest = pr[own_q, :] + pr_rs[0] + pr_rs[1] + pr_rs[2]
        wait_recv(gram_out[1])
        own2 = rest[:, 2 * RANK :] - times_gram(z4, block(gb, 0))
        wait_recv(e3_out)
        z3 = solve(3, own + l3[0], l3[1] + l3[2])
        own2 = own2 - times_gram(z3, block(gb, 1))
        e2[...] = own2
        start(e2_out)
        wait_recv(gram_out[2])
        own10 = rest[:, : 2 * RANK] - times_gram(z4, gc[:, : 2 * RANK])
        own10 = own10 - times_gram(z3, gc[:, 2 * RANK :])
        e10[...] = own10
        start(e10_out)
        start(z_out[3])

        wait_recv(e2_out)
        z2 = solve(2, own2 + l2[1] + l2[2] + l2[3], l2[4] + l2[5] + l2[6] + l2[7])
        wait_recv(e10_out)
        wait_recv(gram_out[3])
        plane = own10 + l2r[0] + l2r[1] + l2r[2] - times_gram(z2, gd[...])
        own1 = plane[:, RANK:]
        e1[...] = own1
        f0[...] = plane[:, :RANK]
        start(e1_out)
        f0_out.start()
        start(z_out[2])

        wait_recv(e1_out)
        z1 = solve(1, own1 + l1[0], l1[1] + l1[2])
        f0_out.wait_recv()
        wait_recv(gram_out[4])
        own0 = plane[:, :RANK] + l1r[...] - times_gram(z1, ge[...])
        e0[...] = own0
        start(e0_out)
        start(z_out[1])
        for level in (4, 3, 2):
            z_wait(level, 1)
        subtract((2, 3, 4))
        wait_recv(e0_out)
        solve(0, own0 + l0[0], l0[1] + l0[2])
        start(z_out[0])
        z_wait(1, 1)
        subtract((1,))
        finish(1)
        for copies in [
            gram_pair, p4_out, p3_out, pr_out, e3_out, e2_out, e10_out, e1_out, [f0_out], e0_out,
        ] + z_out:
            wait_send(copies)

    assert counter[0] <= MESSAGES


MESSAGES = 160


def vmem(*shape, dtype=F32):
    return pltpu.VMEM(shape, dtype)


def tree_solve(loads, inverse, bases, caps):
    rows = loads.shape[0]
    widths = [len(group) * RANK for group in GROUPS]
    q = QUARTER
    scratch = [
        vmem(rows, CASES, dtype=BF16), vmem(rows, rows, dtype=BF16),
        vmem(rows, LEVELS * RANK, dtype=BF16), vmem(*caps.shape, dtype=BF16),
        vmem(rows, CASES), vmem(2 * CASES, LEVELS * RANK),
    ]
    scratch += [vmem(RANK, width) for width in widths] * 2
    scratch += [vmem(3, q, width) for width in widths]
    scratch += [vmem(q, width) for width in widths]
    scratch += [vmem(3, q, widths[3]), vmem(q, 2 * RANK), vmem(q, RANK), vmem(q, RANK), vmem(q, RANK)]
    scratch += [vmem(RANK, width) for width in (RANK, 2 * RANK, 4 * RANK, 2 * RANK, RANK)]
    scratch += [vmem(CASES, width) for width in (RANK, RANK, 3 * RANK)] * 2
    scratch += [vmem(8, q, RANK), vmem(3, q, RANK), vmem(3, q, 3 * RANK)]
    scratch += [vmem(q, RANK), vmem(3, q, RANK), vmem(q, RANK), vmem(8, q, RANK)]
    scratch += [vmem(q, 2 * RANK), vmem(3, q, 2 * RANK), vmem(q, RANK), vmem(3, q, RANK)]
    scratch += [vmem(q, RANK), vmem(q, RANK), vmem(q, RANK), vmem(3, q, RANK)]
    scratch += [vmem(LEVELS, q, RANK), vmem(LEVELS, CASES, RANK)]
    scratch += [
        pltpu.SemaphoreType.DMA((LEVELS + 2,)),
        pltpu.SemaphoreType.DMA((rows // ROWS,)),
        pltpu.SemaphoreType.DMA,
        pltpu.SemaphoreType.DMA((MESSAGES,)),
        pltpu.SemaphoreType.DMA((MESSAGES,)),
    ]
    anywhere = pl.BlockSpec(memory_space=pl.ANY)
    return pl.pallas_call(
        tree_kernel,
        out_shape=(
            jax.ShapeDtypeStruct((rows, CASES), F32),
            jax.ShapeDtypeStruct((CASES, RANK), BF16),
        ),
        in_specs=[anywhere] * 4,
        out_specs=(anywhere, pl.BlockSpec(memory_space=pltpu.VMEM)),
        scratch_shapes=scratch,
        compiler_params=pltpu.CompilerParams(
            collective_id=0, has_side_effects=True, vmem_limit_bytes=50 * 2**20
        ),
        name="tree_solve",
    )(loads, inverse, bases, caps)


def last_kernel(part, basis, z0, out):
    out[...] = part[...] - dot_nt(basis[0], z0[...])


def last_level(part, bases, z0):
    rows = part.shape[0]
    step = rows // 4
    return pl.pallas_call(
        last_kernel,
        grid=(4,),
        out_shape=jax.ShapeDtypeStruct(part.shape, F32),
        in_specs=[
            pl.BlockSpec((step, CASES), lambda i: (i, 0)),
            pl.BlockSpec((1, step, RANK), lambda i: (0, i, 0)),
            pl.BlockSpec((CASES, RANK), lambda i: (0, 0)),
        ],
        out_specs=pl.BlockSpec((step, CASES), lambda i: (i, 0)),
        name="last_level",
    )(part, bases, z0)


def local(loads, leaf_inverse, bases, couplings):
    part, z0 = tree_solve(loads, leaf_inverse, bases, couplings)
    return last_level(part, bases, z0)


def solution(mesh):
    in_specs = (
        P("leaf", None),
        P("leaf", None),
        P(None, "leaf", None),
        P(None, "leaf", None, None),
    )
    return jax.shard_map(
        local, mesh=mesh, in_specs=in_specs, out_specs=P("leaf", None), check_vma=False
    )
```

```python
import jax
import jax.numpy as jnp
from jax import lax
from jax.experimental import pallas as pl
from jax.experimental.pallas import tpu as pltpu
from jax.sharding import PartitionSpec as P

MESH = pl.DeviceIdType.MESH
F32 = jnp.float32
BF16 = jnp.bfloat16
RANK = 128
CASES = 128
LEVELS = 5
QUARTER = CASES // 4
ROWS = 512
TILE = 256


def flip(value, bit):
    return value + bit - 2 * bit * ((value // bit) % 2)


def flips(value, mask):
    for bit in (1, 2, 4):
        if mask & bit:
            value = flip(value, bit)
    return value


def dot_tn(a, b):
    return lax.dot_general(a, b, (((0,), (0,)), ((), ())), preferred_element_type=F32)


def dot_nt(a, b):
    return lax.dot_general(a, b, (((1,), (1,)), ((), ())), preferred_element_type=F32)


def two_parts(value):
    high = value.astype(BF16)
    return high, (value - high.astype(F32)).astype(BF16)


def times_gram(*pairs):
    rows, columns = [], []
    for z, gram in pairs:
        rows += [z, z]
        columns += two_parts(gram)
    return jnp.dot(
        jnp.concatenate(rows, 1), jnp.concatenate(columns, 0), preferred_element_type=F32
    )


GROUPS = (
    ((4, 3),),
    ((4, 2), (3, 2)),
    ((4, 1), (3, 1), (2, 1)),
    ((4, 0), (3, 0), (2, 0), (1, 0)),
)
STARTS = (0, RANK, 3 * RANK, 6 * RANK)
WIDTHS = tuple(len(group) * RANK for group in GROUPS)
PIECES = ((0, 3 * RANK), (3 * RANK, 6 * RANK), (6 * RANK, 10 * RANK))


def tree_kernel(
    loads_hbm, inverse_hbm, bases_hbm, caps_hbm,
    out,
    loads, inverse, bcat, caps, field,
    gram, gram_in, sa_rs, sb_rs, sc_rs, sd_rs,
    s43_own, s42_own, s32_own, s41_own, s321_own, s40_own, s310_own, s32_y, s321_y, s310_y,
    t32_own, t321_own, t320_own, t10_own, t10_z, u10_own,
    g43, g42, g32, g41, g321, g40, g320, g10,
    p4, p3, p2, p10, p4_in, p3_in, p2_in, p10_in, p4_rs, p3_rs, p2_rs, p10_rs,
    e3, l3, e2, l2, h1, k1, h0, k0, d2, m2, e1, l1, f0, l1r, e0, l0,
    zown, zbuf,
    local_sem, chunk_sem, send_sem, recv_sem,
):
    rows = field.shape[0]
    steps = rows // ROWS
    me = lax.axis_index("leaf")
    core = me % 2
    x = (me // 2) % 4
    y = (me // 8) % 4
    z = me // 32

    def device(dx=0, dy=0, dz=0, on=1):
        return ((flips(z, dz) * 4 + flips(y, dy)) * 4 + flips(x, dx)) * 2 + on

    loads_in = []
    for level in range(LEVELS):
        copy = pltpu.make_async_copy(
            bases_hbm.at[level], bcat.at[:, pl.ds(level * RANK, RANK)], local_sem.at[level]
        )
        copy.start()
        loads_in.append(copy)
    loads_copy = pltpu.make_async_copy(loads_hbm, loads, local_sem.at[LEVELS])
    loads_copy.start()
    caps_copy = pltpu.make_async_copy(caps_hbm, caps, local_sem.at[LEVELS + 1])

    def inverse_copy(step):
        part = pl.ds(pl.multiple_of(step * ROWS, ROWS), ROWS)
        return pltpu.make_async_copy(inverse_hbm.at[part], inverse.at[part], chunk_sem.at[step])

    for step in range(steps):
        inverse_copy(step).start()
    caps_copy.start()

    barrier = pltpu.get_barrier_semaphore()

    def greet(partners):
        for partner in partners:
            pl.semaphore_signal(barrier, inc=1, device_id=(partner,), device_id_type=MESH)

    gram_partners = (
        [device(dx=j, on=0) for j in (1, 2, 3)]
        + [device(dy=j, on=0) for j in (1, 2, 3)]
        + [device(dz=1, on=0)]
        + [device(dx=j, on=1) for j in range(4)]
    )
    chain_partners = (
        [device(dx=j, on=0) for j in range(4)]
        + [device(dx=j) for j in (1, 2, 3)]
        + [device(dx=j, dy=1) for j in range(4)]
        + [device(dy=j) for j in (2, 3)]
        + [device(dy=j, dz=1) for j in range(4)]
        + [device(dz=j) for j in (2, 3, 7, 5)]
    )

    @pl.when(core == 0)
    def _():
        greet(gram_partners)

    @pl.when(core == 1)
    def _():
        greet(chain_partners)

    with jax.named_scope("bases_in"):
        for copy in loads_in:
            copy.wait()
    with jax.named_scope("gram_blocks"):
        for level in (4, 3, 2, 1):
            got = dot_tn(bcat[:, level * RANK : (level + 1) * RANK], bcat[:, : level * RANK])
            for begin, group in zip(STARTS, GROUPS):
                for place, (source, target) in enumerate(group):
                    if source == level:
                        at = begin + place * RANK
                        gram[:, at : at + RANK] = got[:, target * RANK : (target + 1) * RANK]

    @pl.when(core == 0)
    def _():
        with jax.named_scope("meet"):
            pl.semaphore_wait(barrier, len(gram_partners))

    @pl.when(core == 1)
    def _():
        with jax.named_scope("meet"):
            pl.semaphore_wait(barrier, len(chain_partners))

    counter = [0]

    class Stage:
        def __init__(self, name, copies, arrive, leave=None):
            self.name = name
            self.number = counter[0]
            counter[0] += 1
            self.copies = copies
            self.arrive = arrive
            self.leave = arrive if leave is None else leave

        def describe(self, src, dst, target):
            return pltpu.make_async_remote_copy(
                src_ref=src, dst_ref=dst,
                send_sem=send_sem.at[self.number], recv_sem=recv_sem.at[self.number],
                device_id=(target,), device_id_type=MESH,
            )

        def start(self):
            for copy in self.copies:
                self.describe(*copy).start()

        def wait_recv(self, arrive=None):
            ref = self.arrive if arrive is None else arrive
            with jax.named_scope("wait_" + self.name):
                self.describe(ref, ref, self.copies[0][2]).wait_recv()

        def wait_send(self):
            self.describe(self.leave, self.leave, self.copies[0][2]).wait_send()

    def quarter(index):
        return pl.ds(pl.multiple_of(index * QUARTER, QUARTER), QUARTER)

    other = device(on=1 - core)
    gram_pair = [
        Stage("gram_in", [(gram.at[:, low:high], gram_in.at[:, low:high], other)], gram_in.at[:, low:high])
        for low, high in PIECES
    ]

    @pl.when(core == 1)
    def _():
        for stage in gram_pair:
            stage.start()

    loads_copy.wait()

    def field_step(step):
        with jax.named_scope("inverse_in"):
            inverse_copy(step).wait()
        with jax.named_scope("field"):
            for begin in range(step * ROWS, (step + 1) * ROWS, TILE):
                part = pl.ds(begin, TILE)
                field[part, :] = jnp.dot(inverse[part, :], loads[...], preferred_element_type=F32)

    field_step(0)

    rs_slots = (sa_rs, sb_rs, sc_rs, sd_rs)
    gram_rs = [
        Stage(
            "gram_row",
            [
                (gram.at[quarter(flips(x, j)), pl.ds(begin, width)], slots.at[j - 1], device(dx=j, on=0))
                for j in (1, 2, 3)
            ],
            slots,
        )
        for begin, width, slots in zip(STARTS, WIDTHS, rs_slots)
    ]

    def pair_sum(piece):
        with jax.named_scope("pair_sums"):
            low, high = PIECES[piece]
            gram_pair[piece].wait_recv()
            gram[:, low:high] += gram_in[:, low:high]

    @pl.when(core == 0)
    def _():
        pair_sum(0)
        gram_rs[0].start()
        gram_rs[1].start()

    field_step(1)

    @pl.when(core == 0)
    def _():
        pair_sum(1)
        gram_rs[2].start()

    field_step(2)

    @pl.when(core == 0)
    def _():
        pair_sum(2)
        gram_rs[3].start()

    for step in range(3, steps):
        field_step(step)

    ordered = (p4, p3, p2, p10)
    with jax.named_scope("projections"):
        field_b = field[...].astype(BF16)
        got = dot_tn(field_b, bcat[:, 3 * RANK :])
        p4[...] = got[:, RANK:]
        p3[...] = got[:, :RANK]
    ordered_in = (p4_in, p3_in, p2_in, p10_in)
    proj_pair = [Stage("proj_in", [(src, dst, other)], dst) for src, dst in zip(ordered, ordered_in)]
    own_q = quarter(x)

    @pl.when(core == 0)
    def _():
        proj_pair[0].start()
        proj_pair[1].start()

    with jax.named_scope("projections_rest"):
        got = dot_tn(field_b, bcat[:, : 3 * RANK])
        p2[...] = got[:, 2 * RANK :]
        p10[...] = got[:, : 2 * RANK]

    z_targets = [(j, on) for on in (0, 1) for j in range(4) if (j, on) != (0, 1)]
    z_out = [
        Stage(
            "z%d" % level,
            [(zown.at[level], zbuf.at[level, own_q], device(dx=j, on=on)) for j, on in z_targets],
            zbuf.at[level], p4_rs,
        )
        for level in range(LEVELS)
    ]

    def z_wait(level, on):
        z_out[level].wait_recv(zbuf.at[level, pl.ds(0, (4 - on) * QUARTER)])

    def subtract(levels, into):
        factors = jnp.concatenate([zbuf[level].astype(BF16) for level in levels], 1)
        low, high = levels[0] * RANK, (levels[-1] + 1) * RANK
        for step in range(steps):
            part = pl.ds(step * ROWS, ROWS)
            into[part, :] = field[part, :] - dot_nt(bcat[part, low:high], factors)

    caps_copy.wait()

    gram_out = {
        name: Stage("gram_" + name, [(src, dst.at[own_q], device(dx=j)) for j in range(4)], dst)
        for name, src, dst in (
            ("43", s43_own, g43), ("42", s42_own, g42), ("32", t32_own, g32), ("41", s41_own, g41),
            ("321", t321_own, g321), ("40", s40_own, g40), ("320", t320_own, g320), ("10", u10_own, g10),
        )
    }
    plane_out = {
        name: Stage("plane" + name, [(src, dst.at[j - 1], device(dy=j, on=0)) for j in (1, 2, 3)], dst)
        for name, src, dst in (("32", s32_own, s32_y), ("321", s321_own, s321_y), ("310", s310_own, s310_y))
    }
    pair_out = Stage("pair", [(t10_own, t10_z, device(dz=1, on=0))], t10_z)

    def row_sum(group):
        gram_rs[group].wait_recv()
        slots = rs_slots[group]
        begin, width = STARTS[group], WIDTHS[group]
        return gram[own_q, begin : begin + width] + slots[0] + slots[1] + slots[2]

    @pl.when(core == 0)
    def _():
        proj_pair[2].start()
        proj_pair[3].start()
        with jax.named_scope("gram_a"):
            s43_own[...] = row_sum(0)
            gram_out["43"].start()
        with jax.named_scope("gram_b"):
            got = row_sum(1)
            s42_own[...] = got[:, :RANK]
            s32_own[...] = got[:, RANK:]
            plane_out["32"].start()
            gram_out["42"].start()
        with jax.named_scope("gram_c"):
            got = row_sum(2)
            s41_own[...] = got[:, :RANK]
            s321_own[...] = got[:, RANK:]
            plane_out["321"].start()
            gram_out["41"].start()
        with jax.named_scope("gram_d"):
            got = row_sum(3)
            s40_own[...] = got[:, :RANK]
            s310_own[...] = got[:, RANK:]
            plane_out["310"].start()
            gram_out["40"].start()
        with jax.named_scope("gram_plane32"):
            plane_out["32"].wait_recv()
            t32_own[:, :RANK] = s32_own[...] + s32_y[0]
            t32_own[:, RANK:] = s32_y[1] + s32_y[2]
            gram_out["32"].start()
        with jax.named_scope("gram_plane321"):
            plane_out["321"].wait_recv()
            near = s321_own[...] + s321_y[0]
            far = s321_y[1] + s321_y[2]
            t321_own[:, :RANK] = near[:, :RANK]
            t321_own[:, RANK : 2 * RANK] = far[:, :RANK]
            t321_own[:, 2 * RANK :] = near[:, RANK:] + far[:, RANK:]
            gram_out["321"].start()
        with jax.named_scope("gram_plane310"):
            plane_out["310"].wait_recv()
            near = s310_own[...] + s310_y[0]
            far = s310_y[1] + s310_y[2]
            total = near[:, RANK:] + far[:, RANK:]
            t10_own[...] = total[:, RANK:]
            pair_out.start()
            t320_own[:, :RANK] = near[:, :RANK]
            t320_own[:, RANK : 2 * RANK] = far[:, :RANK]
            t320_own[:, 2 * RANK :] = total[:, :RANK]
            gram_out["320"].start()
        with jax.named_scope("gram_pair"):
            pair_out.wait_recv()
            u10_own[...] = t10_own[...] + t10_z[...]
            gram_out["10"].start()
        with jax.named_scope("field_update"):
            for level in (4, 3, 2):
                z_wait(level, 0)
            subtract((2, 3, 4), field)
            z_wait(1, 0)
            subtract((1,), field)
            z_wait(0, 0)
            subtract((0,), out)
        with jax.named_scope("sent"):
            for stage in (
                gram_rs + list(gram_out.values()) + list(plane_out.values()) + [pair_out] + proj_pair
            ):
                stage.wait_send()

    def child_side(level):
        return ((y % 2), (y // 2), (z % 2), (z // 2) % 2, (z // 4))[4 - level]

    def solve(level, own, sibling):
        side = child_side(level)
        first = jnp.where(side == 0, own, sibling)
        second = jnp.where(side == 0, sibling, own)
        high, low = two_parts(jnp.concatenate([first, second], 1))
        got = dot_nt(jnp.concatenate([high, low], 0), caps[level, 0])
        rounded = (got[:QUARTER] + got[QUARTER:]).astype(BF16)
        left, right = rounded[:, :RANK], rounded[:, RANK:]
        near = jnp.where(side == 0, left, right)
        far = jnp.where(side == 0, right, left)
        zown[level] = near.astype(F32)
        zbuf[level, own_q, :] = near.astype(F32)
        return near, far

    p4_out = Stage(
        "p4",
        [(p4.at[quarter(flips(x, j))], p4_rs.at[j - 1], device(dx=j)) for j in (1, 2, 3)]
        + [(p4.at[quarter(flips(x, j))], p4_rs.at[3 + j], device(dx=j, dy=1)) for j in range(4)],
        p4_rs,
    )
    p3_out, p2_out, p10_out = [
        Stage(name, [(src.at[quarter(flips(x, j))], slots.at[j - 1], device(dx=j)) for j in (1, 2, 3)], slots)
        for name, src, slots in (("p3", p3, p3_rs), ("p2", p2, p2_rs), ("p10", p10, p10_rs))
    ]
    e3_out = Stage("e3", [(e3, l3.at[j - 1], device(dy=j)) for j in (1, 2, 3)], l3)
    e2_out = Stage("e2", [(e2, l2.at[j - 1], device(dy=j)) for j in (1, 2, 3)], l2)
    h1_out = Stage("h1", [(h1, k1.at[j - 1], device(dy=j)) for j in (1, 2, 3)], k1)
    h0_out = Stage("h0", [(h0, k0.at[j - 1], device(dy=j)) for j in (1, 2, 3)], k0)
    d2_out = Stage("d2", [(d2, m2, device(dz=1))], m2)
    e1_out = Stage("e1", [(e1, l1.at[j - 1], device(dz=j)) for j in (1, 2, 3)], l1)
    f0_out = Stage("f0", [(f0, l1r, device(dz=1))], l1r)
    e0_out = Stage("e0", [(e0, l0.at[i], device(dz=j)) for i, j in enumerate((2, 7, 5))], l0)

    @pl.when(core == 1)
    def _():
        with jax.named_scope("proj_pair"):
            for stage, ref, arrived, onward in zip(
                proj_pair, ordered, ordered_in, (p4_out, p3_out, p2_out, p10_out)
            ):
                stage.wait_recv()
                ref[...] += arrived[...]
                onward.start()

        with jax.named_scope("level4"):
            p4_out.wait_recv()
            own = p4[own_q, :] + p4_rs[0] + p4_rs[1] + p4_rs[2]
            z4, _ = solve(4, own, p4_rs[3] + p4_rs[4] + p4_rs[5] + p4_rs[6])
        with jax.named_scope("correct_by_4"):
            p3_out.wait_recv()
            gram_out["43"].wait_recv()
            own3 = p3[own_q, :] + p3_rs[0] + p3_rs[1] + p3_rs[2] - times_gram((z4, g43[...]))
            e3[...] = own3
            e3_out.start()
            p2_out.wait_recv()
            gram_out["42"].wait_recv()
            own2 = p2[own_q, :] + p2_rs[0] + p2_rs[1] + p2_rs[2] - times_gram((z4, g42[...]))
            e2[...] = own2
            e2_out.start()
            p10_out.wait_recv()
            own10 = p10[own_q, :] + p10_rs[0] + p10_rs[1] + p10_rs[2]
            gram_out["41"].wait_recv()
            own1 = own10[:, RANK:] - times_gram((z4, g41[...]))
            h1[...] = own1
            h1_out.start()
            gram_out["40"].wait_recv()
            own0 = own10[:, :RANK] - times_gram((z4, g40[...]))
            h0[...] = own0
            h0_out.start()
            z_out[4].start()
        with jax.named_scope("level3"):
            e3_out.wait_recv()
            z3, y3 = solve(3, own3 + l3[0], l3[1] + l3[2])
        with jax.named_scope("correct_by_3"):
            e2_out.wait_recv()
            plane2 = own2 + l2[0] + l2[1] + l2[2]
            gram_out["32"].wait_recv()
            plane2 = plane2 - times_gram((z3, g32[:, :RANK]), (y3, g32[:, RANK:]))
            d2[...] = plane2
            d2_out.start()
            z_out[3].start()
            h1_out.wait_recv()
            plane1 = own1 + k1[0] + k1[1] + k1[2]
        with jax.named_scope("level2"):
            d2_out.wait_recv()
            z2, _ = solve(2, plane2, m2[...])
            gram_out["321"].wait_recv()
            plane1 = plane1 - times_gram(
                (z3, g321[:, :RANK]), (y3, g321[:, RANK : 2 * RANK]), (z2, g321[:, 2 * RANK :])
            )
            e1[...] = plane1
            e1_out.start()
        with jax.named_scope("correct_0"):
            h0_out.wait_recv()
            gram_out["320"].wait_recv()
            plane0 = own0 + k0[0] + k0[1] + k0[2] - times_gram(
                (z3, g320[:, :RANK]), (y3, g320[:, RANK : 2 * RANK]), (z2, g320[:, 2 * RANK :])
            )
            f0[...] = plane0
            f0_out.start()
            z_out[2].start()
        with jax.named_scope("level1"):
            e1_out.wait_recv()
            z1, _ = solve(1, plane1 + l1[0], l1[1] + l1[2])
        with jax.named_scope("correct_by_1"):
            f0_out.wait_recv()
            gram_out["10"].wait_recv()
            pair0 = plane0 + l1r[...] - times_gram((z1, g10[...]))
            e0[...] = pair0
            e0_out.start()
            z_out[1].start()
            for level in (4, 3, 2):
                z_wait(level, 1)
            subtract((2, 3, 4), field)
        with jax.named_scope("level0"):
            e0_out.wait_recv()
            solve(0, pair0 + l0[0], l0[1] + l0[2])
            z_out[0].start()
        with jax.named_scope("field_update"):
            z_wait(1, 1)
            subtract((1,), field)
            z_wait(0, 1)
            subtract((0,), out)
        with jax.named_scope("sent"):
            for stage in gram_pair + [
                p4_out, p3_out, p2_out, p10_out, e3_out, e2_out, h1_out, h0_out, d2_out, e1_out, f0_out, e0_out,
            ] + z_out:
                stage.wait_send()

    assert counter[0] == STAGES


STAGES = 40


def vmem(*shape, dtype=F32):
    return pltpu.VMEM(shape, dtype)


def tree_solve(loads, inverse, bases, caps):
    rows = loads.shape[0]
    q = QUARTER
    scratch = [
        vmem(rows, CASES, dtype=BF16), vmem(rows, rows, dtype=BF16),
        vmem(rows, LEVELS * RANK, dtype=BF16), vmem(*caps.shape, dtype=BF16),
        vmem(rows, CASES),
    ]
    scratch += [vmem(RANK, sum(WIDTHS))] * 2
    scratch += [vmem(3, q, width) for width in WIDTHS]
    scratch += [vmem(q, width * RANK) for width in (1, 1, 1, 1, 2, 1, 3)]
    scratch += [vmem(3, q, width * RANK) for width in (1, 2, 3)]
    scratch += [vmem(q, width * RANK) for width in (2, 3, 3, 1, 1, 1)]
    scratch += [vmem(RANK, width * RANK) for width in (1, 1, 2, 1, 3, 1, 3, 1)]
    scratch += [vmem(CASES, width * RANK) for width in (1, 1, 1, 2)] * 2
    scratch += [vmem(7, q, RANK), vmem(3, q, RANK), vmem(3, q, RANK), vmem(3, q, 2 * RANK)]
    scratch += [vmem(q, RANK), vmem(3, q, RANK)] * 4
    scratch += [vmem(q, RANK), vmem(q, RANK)]
    scratch += [vmem(q, RANK), vmem(3, q, RANK), vmem(q, RANK), vmem(q, RANK), vmem(q, RANK), vmem(3, q, RANK)]
    scratch += [vmem(LEVELS, q, RANK), vmem(LEVELS, CASES, RANK)]
    scratch += [
        pltpu.SemaphoreType.DMA((LEVELS + 2,)),
        pltpu.SemaphoreType.DMA((rows // ROWS,)),
        pltpu.SemaphoreType.DMA((STAGES,)),
        pltpu.SemaphoreType.DMA((STAGES,)),
    ]
    anywhere = pl.BlockSpec(memory_space=pl.ANY)
    return pl.pallas_call(
        tree_kernel,
        out_shape=pltpu.VMEM((rows, CASES), F32),
        in_specs=[anywhere] * 4,
        out_specs=pl.BlockSpec(memory_space=pltpu.VMEM),
        scratch_shapes=scratch,
        compiler_params=pltpu.CompilerParams(
            collective_id=0, has_side_effects=True, vmem_limit_bytes=60 * 2**20
        ),
        name="tree_solve",
    )(loads, inverse, bases, caps)


def local(loads, leaf_inverse, bases, couplings):
    return tree_solve(loads, leaf_inverse, bases, couplings)


def solution(mesh):
    in_specs = (
        P("leaf", None),
        P("leaf", None),
        P(None, "leaf", None),
        P(None, "leaf", None, None),
    )
    return jax.shard_map(
        local, mesh=mesh, in_specs=in_specs, out_specs=P("leaf", None), check_vma=False
    )
```

```python
import jax
import jax.numpy as jnp
from jax import lax
from jax.experimental import pallas as pl
from jax.experimental.pallas import tpu as pltpu
from jax.sharding import PartitionSpec as P

MESH = pl.DeviceIdType.MESH
F32 = jnp.float32
BF16 = jnp.bfloat16
RANK = 128
CASES = 128
LEVELS = 5
QUARTER = CASES // 4
ROWS = 512
TILE = 256


def flip(value, bit):
    return value + bit - 2 * bit * ((value // bit) % 2)


def flips(value, mask):
    for bit in (1, 2, 4):
        if mask & bit:
            value = flip(value, bit)
    return value


def dot_tn(a, b):
    return lax.dot_general(a, b, (((0,), (0,)), ((), ())), preferred_element_type=F32)


def dot_nt(a, b):
    return lax.dot_general(a, b, (((1,), (1,)), ((), ())), preferred_element_type=F32)


def two_parts(value):
    high = value.astype(BF16)
    return high, (value - high.astype(F32)).astype(BF16)


def times_gram(*pairs):
    rows, columns = [], []
    for z, gram in pairs:
        rows += [z, z]
        columns += two_parts(gram)
    return jnp.dot(
        jnp.concatenate(rows, 1), jnp.concatenate(columns, 0), preferred_element_type=F32
    )


GROUPS = (
    ((4, 3), (1, 0)),
    ((4, 2), (3, 2)),
    ((4, 1), (3, 1), (2, 1)),
    ((4, 0), (3, 0), (2, 0)),
)
STARTS = (0, 2 * RANK, 4 * RANK, 7 * RANK)
WIDTHS = tuple(len(group) * RANK for group in GROUPS)
PIECES = ((0, 4 * RANK), (4 * RANK, 7 * RANK), (7 * RANK, 10 * RANK))


def tree_kernel(
    loads_hbm, inverse_hbm, bases_hbm, caps_hbm,
    out,
    loads, inverse, bcat, caps, field,
    gram, gram_in, sa_rs, sb_rs, sc_rs, sd_rs,
    s43_own, s42_own, s32_own, s41_own, s321_own, s40_own, s10_own, s320_own, s32_y, s321_y, s10_y, s320_y,
    t32_own, t321_own, t320_own, t10_own, t10_z, u10_own,
    g43, g42, g32, g41, g321, g40, g320, g10,
    p4, p3, p2, p10, p4_in, p3_in, p2_in, p10_in, p4_rs, p3_rs, p2_rs, p10_rs,
    e3, l3, e2, l2, h1, k1, h0, k0, d2, m2, e1, l1, f0, l1r, e0, l0, e0_sent,
    zown, zbuf, z_sent,
    local_sem, chunk_sem, send_sem, recv_sem,
):
    rows = field.shape[0]
    steps = rows // ROWS
    me = lax.axis_index("leaf")
    core = me % 2
    x = (me // 2) % 4
    y = (me // 8) % 4
    z = me // 32

    def device(dx=0, dy=0, dz=0, on=1):
        return ((flips(z, dz) * 4 + flips(y, dy)) * 4 + flips(x, dx)) * 2 + on

    loads_in = []
    for level in range(LEVELS):
        copy = pltpu.make_async_copy(
            bases_hbm.at[level], bcat.at[:, pl.ds(level * RANK, RANK)], local_sem.at[level]
        )
        copy.start()
        loads_in.append(copy)
    loads_copy = pltpu.make_async_copy(loads_hbm, loads, local_sem.at[LEVELS])
    loads_copy.start()
    caps_copy = pltpu.make_async_copy(caps_hbm, caps, local_sem.at[LEVELS + 1])

    def inverse_copy(step):
        part = pl.ds(pl.multiple_of(step * ROWS, ROWS), ROWS)
        return pltpu.make_async_copy(inverse_hbm.at[part], inverse.at[part], chunk_sem.at[step])

    barrier = pltpu.get_barrier_semaphore()

    def greet(partners):
        for partner in partners:
            pl.semaphore_signal(barrier, inc=1, device_id=(partner,), device_id_type=MESH)

    gram_partners = (
        [device(dx=j, on=0) for j in (1, 2, 3)]
        + [device(dy=j, on=0) for j in (1, 2, 3)]
        + [device(dz=j, on=0) for j in (1, 2, 3)]
        + [device(dx=j, on=1) for j in range(4)]
    )
    chain_partners = (
        [device(dx=j, on=0) for j in range(4)]
        + [device(dx=j) for j in (1, 2, 3)]
        + [device(dx=j, dy=1) for j in range(4)]
        + [device(dy=j) for j in (2, 3)]
        + [device(dz=j) for j in (1, 2, 3, 6, 7)]
    )

    @pl.when(core == 0)
    def _():
        greet(gram_partners)

    @pl.when(core == 1)
    def _():
        greet(chain_partners)

    for step in range(steps):
        inverse_copy(step).start()
    caps_copy.start()

    with jax.named_scope("bases_in"):
        for copy in loads_in:
            copy.wait()
    with jax.named_scope("gram_blocks"):
        for level in (4, 3, 2, 1):
            got = dot_tn(bcat[:, level * RANK : (level + 1) * RANK], bcat[:, : level * RANK])
            for begin, group in zip(STARTS, GROUPS):
                for place, (source, target) in enumerate(group):
                    if source == level:
                        at = begin + place * RANK
                        gram[:, at : at + RANK] = got[:, target * RANK : (target + 1) * RANK]

    @pl.when(core == 0)
    def _():
        with jax.named_scope("meet"):
            pl.semaphore_wait(barrier, len(gram_partners))

    @pl.when(core == 1)
    def _():
        with jax.named_scope("meet"):
            pl.semaphore_wait(barrier, len(chain_partners))

    counter = [0]

    class Stage:
        def __init__(self, name, copies, arrive, leave=None):
            self.name = name
            self.number = counter[0]
            counter[0] += 1
            self.copies = copies
            self.arrive = arrive
            self.leave = arrive if leave is None else leave

        def describe(self, src, dst, target):
            return pltpu.make_async_remote_copy(
                src_ref=src, dst_ref=dst,
                send_sem=send_sem, recv_sem=recv_sem.at[self.number],
                device_id=(target,), device_id_type=MESH,
            )

        def start(self):
            for copy in self.copies:
                self.describe(*copy).start()

        def wait_recv(self, arrive=None):
            ref = self.arrive if arrive is None else arrive
            with jax.named_scope("wait_" + self.name):
                self.describe(ref, ref, self.copies[0][2]).wait_recv()

        def wait_send(self):
            self.describe(self.leave, self.leave, self.copies[0][2]).wait_send()

    def quarter(index):
        return pl.ds(pl.multiple_of(index * QUARTER, QUARTER), QUARTER)

    other = device(on=1 - core)
    gram_pair = [
        Stage("gram_in", [(gram.at[:, low:high], gram_in.at[:, low:high], other)], gram_in.at[:, low:high])
        for low, high in PIECES
    ]

    @pl.when(core == 1)
    def _():
        for stage in gram_pair:
            stage.start()

    loads_copy.wait()

    def field_step(step):
        with jax.named_scope("inverse_in"):
            inverse_copy(step).wait()
        with jax.named_scope("field"):
            for begin in range(step * ROWS, (step + 1) * ROWS, TILE):
                part = pl.ds(begin, TILE)
                field[part, :] = jnp.dot(inverse[part, :], loads[...], preferred_element_type=F32)

    field_step(0)

    rs_slots = (sa_rs, sb_rs, sc_rs, sd_rs)
    gram_rs = [
        Stage(
            "gram_row",
            [
                (gram.at[quarter(flips(x, j)), pl.ds(begin, width)], slots.at[j - 1], device(dx=j, on=0))
                for j in (2, 3, 1)
            ],
            slots,
        )
        for begin, width, slots in zip(STARTS, WIDTHS, rs_slots)
    ]

    def pair_sum(piece):
        with jax.named_scope("pair_sums"):
            low, high = PIECES[piece]
            gram_pair[piece].wait_recv()
            gram[:, low:high] += gram_in[:, low:high]

    @pl.when(core == 0)
    def _():
        pair_sum(0)
        gram_rs[0].start()
        gram_rs[1].start()

    field_step(1)

    @pl.when(core == 0)
    def _():
        pair_sum(1)
        gram_rs[2].start()
        pair_sum(2)
        gram_rs[3].start()

    for step in range(2, steps):
        field_step(step)

    ordered = (p4, p3, p2, p10)
    with jax.named_scope("projections"):
        field_b = field[...].astype(BF16)
        got = dot_tn(field_b, bcat[:, 3 * RANK :])
        p4[...] = got[:, RANK:]
        p3[...] = got[:, :RANK]
    ordered_in = (p4_in, p3_in, p2_in, p10_in)
    proj_pair = [Stage("proj_in", [(src, dst, other)], dst) for src, dst in zip(ordered, ordered_in)]
    own_q = quarter(x)

    @pl.when(core == 0)
    def _():
        proj_pair[0].start()
        proj_pair[1].start()

    with jax.named_scope("projection_2"):
        p2[...] = dot_tn(field_b, bcat[:, 2 * RANK : 3 * RANK])

    @pl.when(core == 0)
    def _():
        proj_pair[2].start()

    with jax.named_scope("projections_10"):
        p10[...] = dot_tn(field_b, bcat[:, : 2 * RANK])

    @pl.when(core == 0)
    def _():
        proj_pair[3].start()

    z_targets = [(j, on) for on in (0, 1) for j in (2, 3, 1, 0) if (j, on) != (0, 1)]

    def z_stage(low, high):
        levels = pl.ds(low, high - low)
        return Stage(
            "z%d" % low,
            [
                (zown.at[levels], zbuf.at[levels, own_q], device(dx=j, on=on))
                for j, on in z_targets
            ],
            zbuf.at[levels], z_sent.at[levels],
        )

    z_low, z_one, z_rest = z_stage(0, 1), z_stage(1, 2), z_stage(2, 5)

    def z_wait(stage, low, high, on):
        stage.wait_recv(zbuf.at[pl.ds(low, high - low), pl.ds(0, (4 - on) * QUARTER)])

    def subtract(levels, into):
        factors = jnp.concatenate([zbuf[level].astype(BF16) for level in levels], 1)
        low, high = levels[0] * RANK, (levels[-1] + 1) * RANK
        for step in range(steps):
            part = pl.ds(step * ROWS, ROWS)
            into[part, :] = field[part, :] - dot_nt(bcat[part, low:high], factors)

    caps_copy.wait()

    gram_out = {
        name: Stage("gram_" + name, [(src, dst.at[own_q], device(dx=j)) for j in (2, 3, 1, 0)], dst)
        for name, src, dst in (
            ("43", s43_own, g43), ("42", s42_own, g42), ("32", t32_own, g32), ("41", s41_own, g41),
            ("321", t321_own, g321), ("40", s40_own, g40), ("320", t320_own, g320), ("10", u10_own, g10),
        )
    }
    plane_out = {
        name: Stage("plane" + name, [(src, dst.at[j - 1], device(dy=j, on=0)) for j in (1, 2, 3)], dst)
        for name, src, dst in (("32", s32_own, s32_y), ("321", s321_own, s321_y), ("10", s10_own, s10_y), ("320", s320_own, s320_y))
    }
    pair_out = Stage("pair", [(t10_own, t10_z.at[j - 1], device(dz=j, on=0)) for j in (3, 2, 1)], t10_z)

    def row_sum(group):
        gram_rs[group].wait_recv()
        slots = rs_slots[group]
        begin, width = STARTS[group], WIDTHS[group]
        return gram[own_q, begin : begin + width] + slots[0] + slots[1] + slots[2]

    @pl.when(core == 0)
    def _():
        with jax.named_scope("gram_a"):
            got = row_sum(0)
            s43_own[...] = got[:, :RANK]
            s10_own[...] = got[:, RANK:]
            gram_out["43"].start()
            plane_out["10"].start()
        with jax.named_scope("gram_b"):
            got = row_sum(1)
            s42_own[...] = got[:, :RANK]
            s32_own[...] = got[:, RANK:]
            plane_out["32"].start()
            gram_out["42"].start()
        with jax.named_scope("gram_c"):
            got = row_sum(2)
            s41_own[...] = got[:, :RANK]
            s321_own[...] = got[:, RANK:]
            plane_out["321"].start()
            gram_out["41"].start()
        with jax.named_scope("gram_d"):
            got = row_sum(3)
            s40_own[...] = got[:, :RANK]
            s320_own[...] = got[:, RANK:]
            plane_out["320"].start()
            gram_out["40"].start()
        with jax.named_scope("gram_plane10"):
            plane_out["10"].wait_recv()
            t10_own[...] = s10_own[...] + s10_y[0] + s10_y[1] + s10_y[2]
            pair_out.start()
        with jax.named_scope("gram_plane32"):
            plane_out["32"].wait_recv()
            t32_own[:, :RANK] = s32_own[...] + s32_y[0]
            t32_own[:, RANK:] = s32_y[1] + s32_y[2]
            gram_out["32"].start()
        with jax.named_scope("gram_plane321"):
            plane_out["321"].wait_recv()
            near = s321_own[...] + s321_y[0]
            far = s321_y[1] + s321_y[2]
            t321_own[:, :RANK] = near[:, :RANK]
            t321_own[:, RANK : 2 * RANK] = far[:, :RANK]
            t321_own[:, 2 * RANK :] = near[:, RANK:] + far[:, RANK:]
            gram_out["321"].start()
        with jax.named_scope("gram_plane320"):
            plane_out["320"].wait_recv()
            near = s320_own[...] + s320_y[0]
            far = s320_y[1] + s320_y[2]
            t320_own[:, :RANK] = near[:, :RANK]
            t320_own[:, RANK : 2 * RANK] = far[:, :RANK]
            t320_own[:, 2 * RANK :] = near[:, RANK:] + far[:, RANK:]
            gram_out["320"].start()
        with jax.named_scope("gram_pair"):
            pair_out.wait_recv()
            u10_own[:, :RANK] = t10_own[...] + t10_z[0]
            u10_own[:, RANK:] = t10_z[1] + t10_z[2]
            gram_out["10"].start()
        with jax.named_scope("field_update"):
            z_wait(z_rest, 2, 5, 0)
            z_wait(z_one, 1, 2, 0)
            subtract((1, 2, 3, 4), field)
            z_wait(z_low, 0, 1, 0)
            subtract((0,), out)
        with jax.named_scope("sent"):
            for stage in (
                gram_rs + list(gram_out.values()) + list(plane_out.values()) + [pair_out] + proj_pair
            ):
                stage.wait_send()

    def child_side(level):
        return ((y % 2), (y // 2), (z % 2), (z // 2) % 2, (z // 4))[4 - level]

    def solve(level, own, sibling):
        side = child_side(level)
        first = jnp.where(side == 0, own, sibling)
        second = jnp.where(side == 0, sibling, own)
        high, low = two_parts(jnp.concatenate([first, second], 1))
        got = dot_nt(jnp.concatenate([high, low], 0), caps[level, 0])
        rounded = (got[:QUARTER] + got[QUARTER:]).astype(BF16)
        left, right = rounded[:, :RANK], rounded[:, RANK:]
        near = jnp.where(side == 0, left, right)
        far = jnp.where(side == 0, right, left)
        zown[level] = near.astype(F32)
        zbuf[level, own_q, :] = near.astype(F32)
        return near, far

    p4_out = Stage(
        "p4",
        [(p4.at[quarter(flips(x, j))], p4_rs.at[j - 1], device(dx=j)) for j in (2, 3, 1)]
        + [(p4.at[quarter(flips(x, j))], p4_rs.at[3 + j], device(dx=j, dy=1)) for j in (2, 3, 1, 0)],
        p4_rs,
    )
    p3_out, p2_out, p10_out = [
        Stage(name, [(src.at[quarter(flips(x, j))], slots.at[j - 1], device(dx=j)) for j in (2, 3, 1)], slots)
        for name, src, slots in (("p3", p3, p3_rs), ("p2", p2, p2_rs), ("p10", p10, p10_rs))
    ]
    e3_out = Stage("e3", [(e3, l3.at[j - 1], device(dy=j)) for j in (1, 2, 3)], l3)
    e2_out = Stage("e2", [(e2, l2.at[j - 1], device(dy=j)) for j in (1, 2, 3)], l2)
    h1_out = Stage("h1", [(h1, k1.at[j - 1], device(dy=j)) for j in (1, 2, 3)], k1)
    h0_out = Stage("h0", [(h0, k0.at[j - 1], device(dy=j)) for j in (1, 2, 3)], k0)
    d2_out = Stage("d2", [(d2, m2, device(dz=1))], m2)
    e1_out = Stage("e1", [(e1, l1.at[j - 1], device(dz=j)) for j in (3, 2, 1)], l1)
    f0_out = Stage("f0", [(f0, l1r.at[j - 1], device(dz=j)) for j in (3, 2, 1)], l1r)
    at_end = (z % 4) * (3 - z % 4) == 0
    e0_out = Stage("e0", [(e0, l0, device(dz=j)) for j in (6, 7)], l0, e0_sent)

    @pl.when(core == 1)
    def _():
        with jax.named_scope("proj_pair"):
            for stage, ref, arrived, onward in zip(
                proj_pair, ordered, ordered_in, (p4_out, p3_out, p2_out, p10_out)
            ):
                stage.wait_recv()
                ref[...] += arrived[...]
                onward.start()

        with jax.named_scope("level4"):
            p4_out.wait_recv()
            own = p4[own_q, :] + p4_rs[0] + p4_rs[1] + p4_rs[2]
            z4, _ = solve(4, own, p4_rs[3] + p4_rs[4] + p4_rs[5] + p4_rs[6])
        with jax.named_scope("correct_by_4"):
            p3_out.wait_recv()
            gram_out["43"].wait_recv()
            own3 = p3[own_q, :] + p3_rs[0] + p3_rs[1] + p3_rs[2] - times_gram((z4, g43[...]))
            e3[...] = own3
            e3_out.start()
            p2_out.wait_recv()
            gram_out["42"].wait_recv()
            own2 = p2[own_q, :] + p2_rs[0] + p2_rs[1] + p2_rs[2] - times_gram((z4, g42[...]))
            e2[...] = own2
            e2_out.start()
            p10_out.wait_recv()
            own10 = p10[own_q, :] + p10_rs[0] + p10_rs[1] + p10_rs[2]
            gram_out["41"].wait_recv()
            own1 = own10[:, RANK:] - times_gram((z4, g41[...]))
            h1[...] = own1
            h1_out.start()
            gram_out["40"].wait_recv()
            own0 = own10[:, :RANK] - times_gram((z4, g40[...]))
            h0[...] = own0
            h0_out.start()
        with jax.named_scope("level3"):
            e3_out.wait_recv()
            z3, y3 = solve(3, own3 + l3[0], l3[1] + l3[2])
        with jax.named_scope("correct_by_3"):
            e2_out.wait_recv()
            plane2 = own2 + l2[0] + l2[1] + l2[2]
            gram_out["32"].wait_recv()
            plane2 = plane2 - times_gram((z3, g32[:, :RANK]), (y3, g32[:, RANK:]))
            d2[...] = plane2
            d2_out.start()
            h1_out.wait_recv()
            gram_out["321"].wait_recv()
            plane1 = own1 + k1[0] + k1[1] + k1[2] - times_gram(
                (z3, g321[:, :RANK]), (y3, g321[:, RANK : 2 * RANK])
            )
        with jax.named_scope("level2"):
            d2_out.wait_recv()
            z2, _ = solve(2, plane2, m2[...])
            plane1 = plane1 - times_gram((z2, g321[:, 2 * RANK :]))
            e1[...] = plane1
            e1_out.start()
        with jax.named_scope("correct_0"):
            h0_out.wait_recv()
            gram_out["320"].wait_recv()
            plane0 = own0 + k0[0] + k0[1] + k0[2] - times_gram(
                (z3, g320[:, :RANK]), (y3, g320[:, RANK : 2 * RANK]), (z2, g320[:, 2 * RANK :])
            )
            f0[...] = plane0
            f0_out.start()
            z_rest.start()
        with jax.named_scope("level1"):
            e1_out.wait_recv()
            z1, y1 = solve(1, plane1 + l1[0], l1[1] + l1[2])
        with jax.named_scope("correct_by_1"):
            f0_out.wait_recv()
            near0, far0 = plane0 + l1r[0], l1r[1] + l1r[2]
            gram_out["10"].wait_recv()
            half0 = near0 + far0 - times_gram((z1, g10[:, :RANK]), (y1, g10[:, RANK:]))
            e0[...] = half0

            @pl.when(at_end)
            def _():
                e0_out.start()

            z_one.start()
        with jax.named_scope("level0"):
            e0_out.wait_recv()
            solve(0, half0, l0[...])
            z_low.start()
        with jax.named_scope("field_update"):
            z_wait(z_rest, 2, 5, 1)
            z_wait(z_one, 1, 2, 1)
            subtract((1, 2, 3, 4), field)
            z_wait(z_low, 0, 1, 1)
            subtract((0,), out)
        with jax.named_scope("sent"):
            for stage in gram_pair + [
                p4_out, p3_out, p2_out, p10_out, e3_out, e2_out, h1_out, h0_out, d2_out, e1_out, f0_out,
            ] + [z_rest, z_one, z_low]:
                stage.wait_send()

            @pl.when(at_end)
            def _():
                e0_out.wait_send()

    assert counter[0] == STAGES


STAGES = 39


def vmem(*shape, dtype=F32):
    return pltpu.VMEM(shape, dtype)


def tree_solve(loads, inverse, bases, caps):
    rows = loads.shape[0]
    q = QUARTER
    scratch = [
        vmem(rows, CASES, dtype=BF16), vmem(rows, rows, dtype=BF16),
        vmem(rows, LEVELS * RANK, dtype=BF16), vmem(*caps.shape, dtype=BF16),
        vmem(rows, CASES),
    ]
    scratch += [vmem(RANK, sum(WIDTHS))] * 2
    scratch += [vmem(3, q, width) for width in WIDTHS]
    scratch += [vmem(q, width * RANK) for width in (1, 1, 1, 1, 2, 1, 1, 2)]
    scratch += [vmem(3, q, width * RANK) for width in (1, 2, 1, 2)]
    scratch += [vmem(q, width * RANK) for width in (2, 3, 3, 1)] + [vmem(3, q, RANK), vmem(q, 2 * RANK)]
    scratch += [vmem(RANK, width * RANK) for width in (1, 1, 2, 1, 3, 1, 3, 2)]
    scratch += [vmem(CASES, width * RANK) for width in (1, 1, 1, 2)] * 2
    scratch += [vmem(7, q, RANK), vmem(3, q, RANK), vmem(3, q, RANK), vmem(3, q, 2 * RANK)]
    scratch += [vmem(q, RANK), vmem(3, q, RANK)] * 4
    scratch += [vmem(q, RANK), vmem(q, RANK)]
    scratch += [vmem(q, RANK), vmem(3, q, RANK)] * 2 + [vmem(q, RANK), vmem(q, RANK), vmem(2 * q, RANK)]
    scratch += [vmem(LEVELS, q, RANK), vmem(LEVELS, CASES, RANK), vmem(LEVELS, 7 * q, RANK)]
    scratch += [
        pltpu.SemaphoreType.DMA((LEVELS + 2,)),
        pltpu.SemaphoreType.DMA((rows // ROWS,)),
        pltpu.SemaphoreType.DMA,
        pltpu.SemaphoreType.DMA((STAGES,)),
    ]
    anywhere = pl.BlockSpec(memory_space=pl.ANY)
    return pl.pallas_call(
        tree_kernel,
        out_shape=pltpu.VMEM((rows, CASES), F32),
        in_specs=[anywhere] * 4,
        out_specs=pl.BlockSpec(memory_space=pltpu.VMEM),
        scratch_shapes=scratch,
        compiler_params=pltpu.CompilerParams(
            collective_id=0, has_side_effects=True, vmem_limit_bytes=60 * 2**20
        ),
        name="tree_solve",
    )(loads, inverse, bases, caps)


def local(loads, leaf_inverse, bases, couplings):
    return tree_solve(loads, leaf_inverse, bases, couplings)


def solution(mesh):
    in_specs = (
        P("leaf", None),
        P("leaf", None),
        P(None, "leaf", None),
        P(None, "leaf", None, None),
    )
    return jax.shard_map(
        local, mesh=mesh, in_specs=in_specs, out_specs=P("leaf", None), check_vma=False
    )
```

```python
import jax
import jax.numpy as jnp
from jax import lax
from jax.experimental import pallas as pl
from jax.experimental.pallas import tpu as pltpu
from jax.sharding import PartitionSpec as P

MESH = pl.DeviceIdType.MESH
F32 = jnp.float32
BF16 = jnp.bfloat16
RANK = 128
CASES = 128
LEVELS = 5
QUARTER = CASES // 4
ROWS = 512
TILE = 256


def flip(value, bit):
    return value + bit - 2 * bit * ((value // bit) % 2)


def flips(value, mask):
    for bit in (1, 2, 4):
        if mask & bit:
            value = flip(value, bit)
    return value


def dot_tn(a, b):
    return lax.dot_general(a, b, (((0,), (0,)), ((), ())), preferred_element_type=F32)


def dot_nt(a, b):
    return lax.dot_general(a, b, (((1,), (1,)), ((), ())), preferred_element_type=F32)


def two_parts(value):
    high = value.astype(BF16)
    return high, (value - high.astype(F32)).astype(BF16)


def times_gram(*pairs):
    rows, columns = [], []
    for z, gram in pairs:
        rows += [z, z]
        columns += two_parts(gram)
    return jnp.dot(
        jnp.concatenate(rows, 1), jnp.concatenate(columns, 0), preferred_element_type=F32
    )


GROUPS = (
    ((4, 3), (1, 0)),
    ((4, 2), (3, 2)),
    ((3, 1), (2, 1), (3, 0), (2, 0)),
    ((4, 1), (4, 0)),
)
STARTS = (0, 2 * RANK, 4 * RANK, 8 * RANK)
WIDTHS = tuple(len(group) * RANK for group in GROUPS)
PIECES = ((0, 4 * RANK), (4 * RANK, 8 * RANK), (8 * RANK, 10 * RANK))


def tree_kernel(
    loads_hbm, inverse_hbm, bases_hbm, caps_hbm,
    out,
    loads, inverse, bcat, caps, field,
    gram, gram_in, sa_rs, sb_rs, sc_rs, sd_rs,
    s43_own, s42_own, s32_own, s41_own, s321_own, s40_own, s10_own, s320_own, s32_y, s321_y, s10_y, s320_y,
    t32_own, t321_own, t320_own, t10_own, t10_z, u10_own,
    g43, g42, g32, g41, g321, g40, g320, g10,
    p4, p3, p2, p10, p4_in, p3_in, p2_in, p10_in, p4_rs, p3_rs, p2_rs, p10_rs,
    e3, l3, e2, l2, h1, k1, h0, k0, d2, m2, e1, l1, f0, l1r, e0, l0, e0_sent,
    zown, zbuf, z_sent,
    local_sem, chunk_sem, send_sem, recv_sem,
):
    rows = field.shape[0]
    me = lax.axis_index("leaf")
    core = me % 2
    x = (me // 2) % 4
    y = (me // 8) % 4
    z = me // 32

    def device(dx=0, dy=0, dz=0, on=1):
        return ((flips(z, dz) * 4 + flips(y, dy)) * 4 + flips(x, dx)) * 2 + on

    loads_in = []
    for level in range(LEVELS):
        copy = pltpu.make_async_copy(
            bases_hbm.at[level], bcat.at[:, pl.ds(level * RANK, RANK)], local_sem.at[level]
        )
        copy.start()
        loads_in.append(copy)
    loads_copy = pltpu.make_async_copy(loads_hbm, loads, local_sem.at[LEVELS])
    loads_copy.start()
    caps_copy = pltpu.make_async_copy(caps_hbm, caps, local_sem.at[LEVELS + 1])

    chunks = ((0, rows // 4), (rows // 4, rows // 4), (rows // 2, rows // 2))

    def inverse_copy(step):
        part = pl.ds(*chunks[step])
        return pltpu.make_async_copy(inverse_hbm.at[part], inverse.at[part], chunk_sem.at[step])

    barrier = pltpu.get_barrier_semaphore()

    def greet(partners):
        for partner in partners:
            pl.semaphore_signal(barrier, inc=1, device_id=(partner,), device_id_type=MESH)

    gram_partners = (
        [device(dx=j, on=0) for j in (1, 2, 3)]
        + [device(dy=j, on=0) for j in (1, 2, 3)]
        + [device(dz=j, on=0) for j in (1, 2, 3)]
        + [device(dx=j, on=1) for j in range(4)]
    )
    chain_partners = (
        [device(dx=j, on=0) for j in range(4)]
        + [device(dx=j) for j in (1, 2, 3)]
        + [device(dx=j, dy=1) for j in range(4)]
        + [device(dy=j) for j in (2, 3)]
        + [device(dz=j) for j in (1, 2, 3, 6, 7)]
    )

    @pl.when(core == 0)
    def _():
        greet(gram_partners)

    @pl.when(core == 1)
    def _():
        greet(chain_partners)

    for step in range(len(chunks)):
        inverse_copy(step).start()
    caps_copy.start()

    with jax.named_scope("bases_in"):
        for copy in loads_in:
            copy.wait()
    with jax.named_scope("gram_blocks"):
        for level in (4, 3, 2, 1):
            got = dot_tn(bcat[:, level * RANK : (level + 1) * RANK], bcat[:, : level * RANK])
            for begin, group in zip(STARTS, GROUPS):
                for place, (source, target) in enumerate(group):
                    if source == level:
                        at = begin + place * RANK
                        gram[:, at : at + RANK] = got[:, target * RANK : (target + 1) * RANK]

    @pl.when(core == 0)
    def _():
        with jax.named_scope("meet"):
            pl.semaphore_wait(barrier, len(gram_partners))

    @pl.when(core == 1)
    def _():
        with jax.named_scope("meet"):
            pl.semaphore_wait(barrier, len(chain_partners))

    counter = [0]

    class Stage:
        def __init__(self, name, copies, arrive, leave=None):
            self.name = name
            self.number = counter[0]
            counter[0] += 1
            self.copies = copies
            self.arrive = arrive
            self.leave = arrive if leave is None else leave

        def describe(self, src, dst, target):
            return pltpu.make_async_remote_copy(
                src_ref=src, dst_ref=dst,
                send_sem=send_sem, recv_sem=recv_sem.at[self.number],
                device_id=(target,), device_id_type=MESH,
            )

        def start(self, which=slice(None)):
            for copy in self.copies[which]:
                self.describe(*copy).start()

        def wait_recv(self, arrive=None):
            ref = self.arrive if arrive is None else arrive
            with jax.named_scope("wait_" + self.name):
                self.describe(ref, ref, self.copies[0][2]).wait_recv()

        def wait_send(self):
            self.describe(self.leave, self.leave, self.copies[0][2]).wait_send()

    def quarter(index):
        return pl.ds(pl.multiple_of(index * QUARTER, QUARTER), QUARTER)

    other = device(on=1 - core)
    gram_pair = [
        Stage("gram_in", [(gram.at[:, low:high], gram_in.at[:, low:high], other)], gram_in.at[:, low:high])
        for low, high in PIECES
    ]

    @pl.when(core == 1)
    def _():
        for stage in gram_pair:
            stage.start()

    loads_copy.wait()

    def field_step(step):
        with jax.named_scope("inverse_in"):
            inverse_copy(step).wait()
        with jax.named_scope("field"):
            begin, size = chunks[step]
            for at in range(begin, begin + size, TILE):
                part = pl.ds(at, TILE)
                field[part, :] = jnp.dot(inverse[part, :], loads[...], preferred_element_type=F32)

    field_step(0)

    rs_slots = (sa_rs, sb_rs, sc_rs, sd_rs)
    gram_rs = [
        Stage(
            "gram_row",
            [
                (gram.at[quarter(flips(x, j)), pl.ds(begin, width)], slots.at[j - 1], device(dx=j, on=0))
                for j in (2, 3, 1)
            ],
            slots,
        )
        for begin, width, slots in zip(STARTS, WIDTHS, rs_slots)
    ]

    def pair_sum(piece):
        with jax.named_scope("pair_sums"):
            low, high = PIECES[piece]
            gram_pair[piece].wait_recv()
            gram[:, low:high] += gram_in[:, low:high]

    @pl.when(core == 0)
    def _():
        pair_sum(0)
        gram_rs[0].start()
        gram_rs[1].start()

    field_step(1)

    @pl.when(core == 0)
    def _():
        pair_sum(1)
        gram_rs[2].start()

    field_step(2)

    ordered = (p4, p3, p2, p10)
    with jax.named_scope("projections"):
        field_b = field[...].astype(BF16)
        got = dot_tn(field_b, bcat[:, 3 * RANK :])
        p4[...] = got[:, RANK:]
        p3[...] = got[:, :RANK]
    ordered_in = (p4_in, p3_in, p2_in, p10_in)
    proj_pair = [Stage("proj_in", [(src, dst, other)], dst) for src, dst in zip(ordered, ordered_in)]
    own_q = quarter(x)

    @pl.when(core == 0)
    def _():
        proj_pair[0].start()
        proj_pair[1].start()

    with jax.named_scope("projection_2"):
        p2[...] = dot_tn(field_b, bcat[:, 2 * RANK : 3 * RANK])

    @pl.when(core == 0)
    def _():
        proj_pair[2].start()
        pair_sum(2)
        gram_rs[3].start()

    with jax.named_scope("projections_10"):
        p10[...] = dot_tn(field_b, bcat[:, : 2 * RANK])

    @pl.when(core == 0)
    def _():
        proj_pair[3].start()

    z_targets = [(j, on) for on in (0, 1) for j in (2, 3, 1, 0) if (j, on) != (0, 1)]

    def z_stage(low, high):
        levels = pl.ds(low, high - low)
        return Stage(
            "z%d" % low,
            [
                (zown.at[levels], zbuf.at[levels, own_q], device(dx=j, on=on))
                for j, on in z_targets
            ],
            zbuf.at[levels], z_sent.at[levels],
        )

    z_low, z_one, z_rest = z_stage(0, 1), z_stage(1, 2), z_stage(2, 5)

    def z_wait(stage, low, high, on):
        stage.wait_recv(zbuf.at[pl.ds(low, high - low), pl.ds(0, (4 - on) * QUARTER)])

    def subtract(levels, into):
        factors = jnp.concatenate([zbuf[level].astype(BF16) for level in levels], 1)
        low, high = levels[0] * RANK, (levels[-1] + 1) * RANK
        for begin in range(0, rows, ROWS):
            part = pl.ds(begin, ROWS)
            into[part, :] = field[part, :] - dot_nt(bcat[part, low:high], factors)

    caps_copy.wait()

    gram_out = {
        name: Stage("gram_" + name, [(src, dst.at[own_q], device(dx=j)) for j in (2, 3, 1, 0)], dst)
        for name, src, dst in (
            ("43", s43_own, g43), ("42", s42_own, g42), ("32", t32_own, g32), ("41", s41_own, g41),
            ("321", t321_own, g321), ("40", s40_own, g40), ("320", t320_own, g320), ("10", u10_own, g10),
        )
    }
    plane_out = {
        name: Stage("plane" + name, [(src, dst.at[j - 1], device(dy=j, on=0)) for j in (1, 2, 3)], dst)
        for name, src, dst in (("32", s32_own, s32_y), ("321", s321_own, s321_y), ("10", s10_own, s10_y), ("320", s320_own, s320_y))
    }
    pair_out = Stage("pair", [(t10_own, t10_z.at[j - 1], device(dz=j, on=0)) for j in (3, 2, 1)], t10_z)

    def row_sum(group):
        gram_rs[group].wait_recv()
        slots = rs_slots[group]
        begin, width = STARTS[group], WIDTHS[group]
        return gram[own_q, begin : begin + width] + slots[0] + slots[1] + slots[2]

    @pl.when(core == 0)
    def _():
        with jax.named_scope("gram_a"):
            got = row_sum(0)
            s43_own[...] = got[:, :RANK]
            s10_own[...] = got[:, RANK:]
            gram_out["43"].start()
            plane_out["10"].start()
        with jax.named_scope("gram_b"):
            got = row_sum(1)
            s42_own[...] = got[:, :RANK]
            s32_own[...] = got[:, RANK:]
            plane_out["32"].start()
            gram_out["42"].start()
        with jax.named_scope("gram_c"):
            got = row_sum(2)
            s321_own[...] = got[:, : 2 * RANK]
            s320_own[...] = got[:, 2 * RANK :]
            plane_out["321"].start()
            plane_out["320"].start()
        with jax.named_scope("gram_d"):
            got = row_sum(3)
            s41_own[...] = got[:, :RANK]
            s40_own[...] = got[:, RANK:]
            gram_out["41"].start()
            gram_out["40"].start()
        with jax.named_scope("gram_plane10"):
            plane_out["10"].wait_recv()
            t10_own[...] = s10_own[...] + s10_y[0] + s10_y[1] + s10_y[2]
            pair_out.start()
        with jax.named_scope("gram_plane32"):
            plane_out["32"].wait_recv()
            t32_own[:, :RANK] = s32_own[...] + s32_y[0]
            t32_own[:, RANK:] = s32_y[1] + s32_y[2]
            gram_out["32"].start()
        with jax.named_scope("gram_plane321"):
            plane_out["321"].wait_recv()
            near = s321_own[...] + s321_y[0]
            far = s321_y[1] + s321_y[2]
            t321_own[:, :RANK] = near[:, :RANK]
            t321_own[:, RANK : 2 * RANK] = far[:, :RANK]
            t321_own[:, 2 * RANK :] = near[:, RANK:] + far[:, RANK:]
            gram_out["321"].start()
        with jax.named_scope("gram_plane320"):
            plane_out["320"].wait_recv()
            near = s320_own[...] + s320_y[0]
            far = s320_y[1] + s320_y[2]
            t320_own[:, :RANK] = near[:, :RANK]
            t320_own[:, RANK : 2 * RANK] = far[:, :RANK]
            t320_own[:, 2 * RANK :] = near[:, RANK:] + far[:, RANK:]
            gram_out["320"].start()
        with jax.named_scope("gram_pair"):
            pair_out.wait_recv()
            u10_own[:, :RANK] = t10_own[...] + t10_z[0]
            u10_own[:, RANK:] = t10_z[1] + t10_z[2]
            gram_out["10"].start()
        with jax.named_scope("field_update"):
            z_wait(z_rest, 2, 5, 0)
            z_wait(z_one, 1, 2, 0)
            subtract((1, 2, 3, 4), field)
            z_wait(z_low, 0, 1, 0)
            subtract((0,), out)
        with jax.named_scope("sent"):
            for stage in (
                gram_rs + list(gram_out.values()) + list(plane_out.values()) + [pair_out] + proj_pair
            ):
                stage.wait_send()

    def child_side(level):
        return ((y % 2), (y // 2), (z % 2), (z // 2) % 2, (z // 4))[4 - level]

    def solve(level, own, sibling):
        side = child_side(level)
        first = jnp.where(side == 0, own, sibling)
        second = jnp.where(side == 0, sibling, own)
        high, low = two_parts(jnp.concatenate([first, second], 1))
        got = dot_nt(jnp.concatenate([high, low], 0), caps[level, 0])
        rounded = (got[:QUARTER] + got[QUARTER:]).astype(BF16)
        left, right = rounded[:, :RANK], rounded[:, RANK:]
        near = jnp.where(side == 0, left, right)
        far = jnp.where(side == 0, right, left)
        zown[level] = near.astype(F32)
        zbuf[level, own_q, :] = near.astype(F32)
        return near, far

    p4_out = Stage(
        "p4",
        [(p4.at[quarter(flips(x, j))], p4_rs.at[j - 1], device(dx=j)) for j in (2, 3, 1)]
        + [(p4.at[quarter(flips(x, j))], p4_rs.at[3 + j], device(dx=j, dy=1)) for j in (2, 3, 1, 0)],
        p4_rs,
    )
    p3_out, p2_out, p10_out = [
        Stage(name, [(src.at[quarter(flips(x, j))], slots.at[j - 1], device(dx=j)) for j in (2, 3, 1)], slots)
        for name, src, slots in (("p3", p3, p3_rs), ("p2", p2, p2_rs), ("p10", p10, p10_rs))
    ]
    e3_out = Stage("e3", [(e3, l3.at[j - 1], device(dy=j)) for j in (1, 2, 3)], l3)
    e2_out = Stage("e2", [(e2, l2.at[j - 1], device(dy=j)) for j in (1, 2, 3)], l2)
    h1_out = Stage("h1", [(h1, k1.at[j - 1], device(dy=j)) for j in (1, 2, 3)], k1)
    h0_out = Stage("h0", [(h0, k0.at[j - 1], device(dy=j)) for j in (1, 2, 3)], k0)
    d2_out = Stage("d2", [(d2, m2, device(dz=1))], m2)
    e1_out = Stage("e1", [(e1, l1.at[j - 1], device(dz=j)) for j in (3, 2, 1)], l1)
    f0_out = Stage("f0", [(f0, l1r.at[j - 1], device(dz=j)) for j in (3, 2, 1)], l1r)
    at_end = (z % 4) * (3 - z % 4) == 0
    inside = (z % 4) * (3 - z % 4) != 0

    def ends_first(stage):
        @pl.when(at_end)
        def _():
            stage.start(slice(0, 1))

        @pl.when(inside)
        def _():
            stage.start(slice(1, 3))

    def the_others(stages):
        @pl.when(at_end)
        def _():
            for stage in stages:
                stage.start(slice(1, 3))

        @pl.when(inside)
        def _():
            for stage in stages:
                stage.start(slice(0, 1))

    e0_out = Stage("e0", [(e0, l0, device(dz=j)) for j in (6, 7)], l0, e0_sent)

    @pl.when(core == 1)
    def _():
        with jax.named_scope("proj_pair"):
            for stage, ref, arrived, onward in zip(
                proj_pair, ordered, ordered_in, (p4_out, p3_out, p2_out, p10_out)
            ):
                stage.wait_recv()
                ref[...] += arrived[...]
                onward.start()

        with jax.named_scope("level4"):
            p4_out.wait_recv()
            own = p4[own_q, :] + p4_rs[0] + p4_rs[1] + p4_rs[2]
            z4, _ = solve(4, own, p4_rs[3] + p4_rs[4] + p4_rs[5] + p4_rs[6])
        with jax.named_scope("correct_by_4"):
            p3_out.wait_recv()
            gram_out["43"].wait_recv()
            own3 = p3[own_q, :] + p3_rs[0] + p3_rs[1] + p3_rs[2] - times_gram((z4, g43[...]))
            e3[...] = own3
            e3_out.start()
            p2_out.wait_recv()
            gram_out["42"].wait_recv()
            own2 = p2[own_q, :] + p2_rs[0] + p2_rs[1] + p2_rs[2] - times_gram((z4, g42[...]))
            e2[...] = own2
            e2_out.start()
            p10_out.wait_recv()
            own10 = p10[own_q, :] + p10_rs[0] + p10_rs[1] + p10_rs[2]
            gram_out["41"].wait_recv()
            own1 = own10[:, RANK:] - times_gram((z4, g41[...]))
            h1[...] = own1
            h1_out.start()
            gram_out["40"].wait_recv()
            own0 = own10[:, :RANK] - times_gram((z4, g40[...]))
            h0[...] = own0
            h0_out.start()
        with jax.named_scope("level3"):
            e3_out.wait_recv()
            z3, y3 = solve(3, own3 + l3[0], l3[1] + l3[2])
        with jax.named_scope("correct_by_3"):
            e2_out.wait_recv()
            plane2 = own2 + l2[0] + l2[1] + l2[2]
            gram_out["32"].wait_recv()
            plane2 = plane2 - times_gram((z3, g32[:, :RANK]), (y3, g32[:, RANK:]))
            d2[...] = plane2
            d2_out.start()
            h1_out.wait_recv()
            gram_out["321"].wait_recv()
            plane1 = own1 + k1[0] + k1[1] + k1[2] - times_gram(
                (z3, g321[:, :RANK]), (y3, g321[:, RANK : 2 * RANK])
            )
        with jax.named_scope("level2"):
            d2_out.wait_recv()
            z2, _ = solve(2, plane2, m2[...])
            plane1 = plane1 - times_gram((z2, g321[:, 2 * RANK :]))
            e1[...] = plane1
            ends_first(e1_out)
        with jax.named_scope("correct_0"):
            h0_out.wait_recv()
            gram_out["320"].wait_recv()
            plane0 = own0 + k0[0] + k0[1] + k0[2] - times_gram(
                (z3, g320[:, :RANK]), (y3, g320[:, RANK : 2 * RANK]), (z2, g320[:, 2 * RANK :])
            )
            f0[...] = plane0
            ends_first(f0_out)
            the_others((e1_out, f0_out))
            z_rest.start()
        with jax.named_scope("level1"):
            e1_out.wait_recv()
            z1, y1 = solve(1, plane1 + l1[0], l1[1] + l1[2])
        with jax.named_scope("correct_by_1"):
            f0_out.wait_recv()
            near0, far0 = plane0 + l1r[0], l1r[1] + l1r[2]
            gram_out["10"].wait_recv()
            half0 = near0 + far0 - times_gram((z1, g10[:, :RANK]), (y1, g10[:, RANK:]))
            e0[...] = half0

            @pl.when(at_end)
            def _():
                e0_out.start()

            z_one.start()
        with jax.named_scope("level0"):
            e0_out.wait_recv()
            solve(0, half0, l0[...])
            z_low.start()
        with jax.named_scope("field_update"):
            z_wait(z_rest, 2, 5, 1)
            z_wait(z_one, 1, 2, 1)
            subtract((1, 2, 3, 4), field)
            z_wait(z_low, 0, 1, 1)
            subtract((0,), out)
        with jax.named_scope("sent"):
            for stage in gram_pair + [
                p4_out, p3_out, p2_out, p10_out, e3_out, e2_out, h1_out, h0_out, d2_out, e1_out, f0_out,
            ] + [z_rest, z_one, z_low]:
                stage.wait_send()

            @pl.when(at_end)
            def _():
                e0_out.wait_send()

    assert counter[0] == STAGES


STAGES = 39


def vmem(*shape, dtype=F32):
    return pltpu.VMEM(shape, dtype)


def tree_solve(loads, inverse, bases, caps):
    rows = loads.shape[0]
    q = QUARTER
    scratch = [
        vmem(rows, CASES, dtype=BF16), vmem(rows, rows, dtype=BF16),
        vmem(rows, LEVELS * RANK, dtype=BF16), vmem(*caps.shape, dtype=BF16),
        vmem(rows, CASES),
    ]
    scratch += [vmem(RANK, sum(WIDTHS))] * 2
    scratch += [vmem(3, q, width) for width in WIDTHS]
    scratch += [vmem(q, width * RANK) for width in (1, 1, 1, 1, 2, 1, 1, 2)]
    scratch += [vmem(3, q, width * RANK) for width in (1, 2, 1, 2)]
    scratch += [vmem(q, width * RANK) for width in (2, 3, 3, 1)] + [vmem(3, q, RANK), vmem(q, 2 * RANK)]
    scratch += [vmem(RANK, width * RANK) for width in (1, 1, 2, 1, 3, 1, 3, 2)]
    scratch += [vmem(CASES, width * RANK) for width in (1, 1, 1, 2)] * 2
    scratch += [vmem(7, q, RANK), vmem(3, q, RANK), vmem(3, q, RANK), vmem(3, q, 2 * RANK)]
    scratch += [vmem(q, RANK), vmem(3, q, RANK)] * 4
    scratch += [vmem(q, RANK), vmem(q, RANK)]
    scratch += [vmem(q, RANK), vmem(3, q, RANK)] * 2 + [vmem(q, RANK), vmem(q, RANK), vmem(2 * q, RANK)]
    scratch += [vmem(LEVELS, q, RANK), vmem(LEVELS, CASES, RANK), vmem(LEVELS, 7 * q, RANK)]
    scratch += [
        pltpu.SemaphoreType.DMA((LEVELS + 2,)),
        pltpu.SemaphoreType.DMA((3,)),
        pltpu.SemaphoreType.DMA,
        pltpu.SemaphoreType.DMA((STAGES,)),
    ]
    anywhere = pl.BlockSpec(memory_space=pl.ANY)
    return pl.pallas_call(
        tree_kernel,
        out_shape=pltpu.VMEM((rows, CASES), F32),
        in_specs=[anywhere] * 4,
        out_specs=pl.BlockSpec(memory_space=pltpu.VMEM),
        scratch_shapes=scratch,
        compiler_params=pltpu.CompilerParams(
            collective_id=0, has_side_effects=True, vmem_limit_bytes=60 * 2**20
        ),
        name="tree_solve",
    )(loads, inverse, bases, caps)


def local(loads, leaf_inverse, bases, couplings):
    return tree_solve(loads, leaf_inverse, bases, couplings)


def solution(mesh):
    in_specs = (
        P("leaf", None),
        P("leaf", None),
        P(None, "leaf", None),
        P(None, "leaf", None, None),
    )
    return jax.shard_map(
        local, mesh=mesh, in_specs=in_specs, out_specs=P("leaf", None), check_vma=False
    )
```

```python
import jax
import jax.numpy as jnp
from jax import lax
from jax.experimental import pallas as pl
from jax.experimental.pallas import tpu as pltpu
from jax.sharding import PartitionSpec as P

MESH = pl.DeviceIdType.MESH
F32 = jnp.float32
BF16 = jnp.bfloat16
RANK = 128
CASES = 128
LEVELS = 5
QUARTER = CASES // 4
ROWS = 512
TILE = 256


def flip(value, bit):
    return value + bit - 2 * bit * ((value // bit) % 2)


def flips(value, mask):
    for bit in (1, 2, 4):
        if mask & bit:
            value = flip(value, bit)
    return value


def dot_tn(a, b):
    return lax.dot_general(a, b, (((0,), (0,)), ((), ())), preferred_element_type=F32)


def dot_nt(a, b):
    return lax.dot_general(a, b, (((1,), (1,)), ((), ())), preferred_element_type=F32)


def two_parts(value):
    high = value.astype(BF16)
    return high, (value - high.astype(F32)).astype(BF16)


def times_gram(*pairs):
    rows, columns = [], []
    for z, gram in pairs:
        rows += [z, z]
        columns += two_parts(gram)
    return jnp.dot(
        jnp.concatenate(rows, 1), jnp.concatenate(columns, 0), preferred_element_type=F32
    )


GROUPS = (
    ((4, 3), (1, 0)),
    ((2, 1), (2, 0)),
    ((4, 2), (3, 2)),
    ((3, 1), (3, 0)),
    ((4, 1), (4, 0)),
)
WIDTH = 2 * RANK
STARTS = tuple(WIDTH * at for at in range(len(GROUPS)))
PIECES = ((0, 2 * WIDTH), (2 * WIDTH, 4 * WIDTH), (4 * WIDTH, 5 * WIDTH))


def tree_kernel(
    loads_hbm, inverse_hbm, bases_hbm, caps_hbm,
    out,
    loads, inverse, bcat, caps, field,
    gram, gram_in, s0_rs, s1_rs, s2_rs, s3_rs, s4_rs,
    s43_own, s10_own, s42_own, s32_own, s31_own, s30_own, s41_own, s40_own, s32_y, s31_y, s30_y, s10_y,
    plane_own, plane_x, t32_own, t31_own, t30_own, t2_own, t10_own, t10_z, u10_own,
    g43, g42, g32, g41, g31, g40, g30, g2, g10,
    p4, p3, p2, p10, p4_in, p3_in, p2_in, p10_in, p4_rs, p3_rs, p2_rs, p10_rs,
    e3, l3, e2, l2, h1, k1, h0, k0, d2, m2, e1, l1, f0, l1r, e0, l0, e0_sent,
    zown, zbuf, z_sent,
    local_sem, chunk_sem, send_sem, recv_sem,
):
    rows = field.shape[0]
    me = lax.axis_index("leaf")
    core = me % 2
    x = (me // 2) % 4
    y = (me // 8) % 4
    z = me // 32

    def device(dx=0, dy=0, dz=0, on=1):
        return ((flips(z, dz) * 4 + flips(y, dy)) * 4 + flips(x, dx)) * 2 + on

    loads_in = []
    for level in range(LEVELS):
        copy = pltpu.make_async_copy(
            bases_hbm.at[level], bcat.at[:, pl.ds(level * RANK, RANK)], local_sem.at[level]
        )
        copy.start()
        loads_in.append(copy)
    loads_copy = pltpu.make_async_copy(loads_hbm, loads, local_sem.at[LEVELS])
    loads_copy.start()
    caps_copy = pltpu.make_async_copy(caps_hbm, caps, local_sem.at[LEVELS + 1])

    chunks = ((0, rows // 4), (rows // 4, rows // 4), (rows // 2, rows // 2))

    def inverse_copy(step):
        part = pl.ds(*chunks[step])
        return pltpu.make_async_copy(inverse_hbm.at[part], inverse.at[part], chunk_sem.at[step])

    barrier = pltpu.get_barrier_semaphore()

    def greet(partners):
        for partner in partners:
            pl.semaphore_signal(barrier, inc=1, device_id=(partner,), device_id_type=MESH)

    gram_partners = (
        [device(dx=j, on=0) for j in (1, 2, 3)]
        + [device(dy=j, on=0) for j in (1, 2, 3)]
        + [device(dz=j, on=0) for j in (1, 2, 3)]
        + [device(dx=j, on=1) for j in range(4)]
        + [device(dy=j, on=1) for j in (1, 2, 3)]
    )
    chain_partners = (
        [device(dx=j, on=0) for j in range(4)]
        + [device(dy=j, on=0) for j in (1, 2, 3)]
        + [device(dx=j) for j in (1, 2, 3)]
        + [device(dx=j, dy=1) for j in range(4)]
        + [device(dy=j) for j in (2, 3)]
        + [device(dz=j) for j in (1, 2, 3, 6, 7)]
    )

    @pl.when(core == 0)
    def _():
        greet(gram_partners)

    @pl.when(core == 1)
    def _():
        greet(chain_partners)

    for step in range(len(chunks)):
        inverse_copy(step).start()
    caps_copy.start()

    with jax.named_scope("bases_in"):
        for copy in loads_in:
            copy.wait()
    with jax.named_scope("gram_blocks"):
        for level in (4, 3, 2, 1):
            got = dot_tn(bcat[:, level * RANK : (level + 1) * RANK], bcat[:, : level * RANK])
            for begin, group in zip(STARTS, GROUPS):
                for place, (source, target) in enumerate(group):
                    if source == level:
                        at = begin + place * RANK
                        gram[:, at : at + RANK] = got[:, target * RANK : (target + 1) * RANK]

    @pl.when(core == 0)
    def _():
        with jax.named_scope("meet"):
            pl.semaphore_wait(barrier, len(gram_partners))

    @pl.when(core == 1)
    def _():
        with jax.named_scope("meet"):
            pl.semaphore_wait(barrier, len(chain_partners))

    counter = [0]

    class Stage:
        def __init__(self, name, copies, arrive, leave=None):
            self.name = name
            self.number = counter[0]
            counter[0] += 1
            self.copies = copies
            self.arrive = arrive
            self.leave = arrive if leave is None else leave

        def describe(self, src, dst, target):
            return pltpu.make_async_remote_copy(
                src_ref=src, dst_ref=dst,
                send_sem=send_sem, recv_sem=recv_sem.at[self.number],
                device_id=(target,), device_id_type=MESH,
            )

        def start(self, which=slice(None)):
            for copy in self.copies[which]:
                self.describe(*copy).start()

        def wait_recv(self, arrive=None):
            ref = self.arrive if arrive is None else arrive
            with jax.named_scope("wait_" + self.name):
                self.describe(ref, ref, self.copies[0][2]).wait_recv()

        def wait_send(self):
            self.describe(self.leave, self.leave, self.copies[0][2]).wait_send()

    def quarter(index):
        return pl.ds(pl.multiple_of(index * QUARTER, QUARTER), QUARTER)

    other = device(on=1 - core)
    gram_pair = [
        Stage("gram_in", [(gram.at[:, low:high], gram_in.at[:, low:high], other)], gram_in.at[:, low:high])
        for low, high in PIECES
    ]

    @pl.when(core == 1)
    def _():
        for stage in gram_pair:
            stage.start()

    loads_copy.wait()

    def field_step(step):
        with jax.named_scope("inverse_in"):
            inverse_copy(step).wait()
        with jax.named_scope("field"):
            begin, size = chunks[step]
            for at in range(begin, begin + size, TILE):
                part = pl.ds(at, TILE)
                field[part, :] = jnp.dot(inverse[part, :], loads[...], preferred_element_type=F32)

    field_step(0)

    rs_slots = (s0_rs, s1_rs, s2_rs, s3_rs, s4_rs)

    def deal(group):
        columns, slots = pl.ds(STARTS[group], WIDTH), rs_slots[group]
        if group == 1:
            copies = [
                (gram.at[quarter(flips(y, j)), columns], slots.at[j - 1], device(dy=j, on=0))
                for j in (2, 3, 1)
            ]
        else:
            copies = [
                (gram.at[quarter(flips(x, j)), columns], slots.at[j - 1], device(dx=j, on=0))
                for j in (2, 3, 1)
            ]
        return Stage("gram_row%d" % group, copies, slots)

    gram_rs = [deal(group) for group in range(len(GROUPS))]

    def pair_sum(piece):
        with jax.named_scope("pair_sums"):
            low, high = PIECES[piece]
            gram_pair[piece].wait_recv()
            gram[:, low:high] += gram_in[:, low:high]

    @pl.when(core == 0)
    def _():
        pair_sum(0)
        gram_rs[0].start()
        gram_rs[1].start()

    field_step(1)

    @pl.when(core == 0)
    def _():
        pair_sum(1)
        gram_rs[2].start()
        gram_rs[3].start()

    field_step(2)

    ordered = (p4, p3, p2, p10)
    with jax.named_scope("projections"):
        field_b = field[...].astype(BF16)
        got = dot_tn(field_b, bcat[:, 3 * RANK :])
        p4[...] = got[:, RANK:]
        p3[...] = got[:, :RANK]
    ordered_in = (p4_in, p3_in, p2_in, p10_in)
    proj_pair = [Stage("proj_in", [(src, dst, other)], dst) for src, dst in zip(ordered, ordered_in)]
    own_q = quarter(x)

    @pl.when(core == 0)
    def _():
        proj_pair[0].start()
        proj_pair[1].start()

    with jax.named_scope("projection_2"):
        p2[...] = dot_tn(field_b, bcat[:, 2 * RANK : 3 * RANK])

    @pl.when(core == 0)
    def _():
        proj_pair[2].start()
        pair_sum(2)
        gram_rs[4].start()

    with jax.named_scope("projections_10"):
        p10[...] = dot_tn(field_b, bcat[:, : 2 * RANK])

    @pl.when(core == 0)
    def _():
        proj_pair[3].start()

    z_targets = [(j, on) for on in (0, 1) for j in (2, 3, 1, 0) if (j, on) != (0, 1)]

    def z_stage(low, high):
        levels = pl.ds(low, high - low)
        return Stage(
            "z%d" % low,
            [
                (zown.at[levels], zbuf.at[levels, own_q], device(dx=j, on=on))
                for j, on in z_targets
            ],
            zbuf.at[levels], z_sent.at[levels],
        )

    z_low, z_one, z_rest = z_stage(0, 1), z_stage(1, 2), z_stage(2, 5)

    def z_wait(stage, low, high, on):
        stage.wait_recv(zbuf.at[pl.ds(low, high - low), pl.ds(0, (4 - on) * QUARTER)])

    def subtract(levels, into):
        factors = jnp.concatenate([zbuf[level].astype(BF16) for level in levels], 1)
        low, high = levels[0] * RANK, (levels[-1] + 1) * RANK
        for begin in range(0, rows, ROWS):
            part = pl.ds(begin, ROWS)
            into[part, :] = field[part, :] - dot_nt(bcat[part, low:high], factors)

    caps_copy.wait()

    own_y = quarter(y)
    gram_out = {
        name: Stage("gram_" + name, [(src, dst.at[own_q], device(dx=j)) for j in (2, 3, 1, 0)], dst)
        for name, src, dst in (
            ("43", s43_own, g43), ("42", s42_own, g42), ("32", t32_own, g32), ("41", s41_own, g41),
            ("31", t31_own, g31), ("40", s40_own, g40), ("30", t30_own, g30), ("10", u10_own, g10),
        )
    }
    gram_out["2"] = Stage("gram_2", [(t2_own, g2.at[own_y], device(dy=j)) for j in (2, 3, 1, 0)], g2)
    column_out = {
        name: Stage("column" + name, [(src, dst.at[j - 1], device(dy=j, on=0)) for j in (2, 3, 1)], dst)
        for name, src, dst in (
            ("32", s32_own, s32_y), ("31", s31_own, s31_y), ("30", s30_own, s30_y), ("10", s10_own, s10_y),
        )
    }
    plane_out = Stage(
        "plane", [(plane_own, plane_x.at[j - 1], device(dx=j, on=0)) for j in (2, 3, 1)], plane_x
    )
    pair_out = Stage("pair", [(t10_own, t10_z.at[j - 1], device(dz=j, on=0)) for j in (3, 2, 1)], t10_z)

    def dealt(group, rows_own):
        gram_rs[group].wait_recv()
        slots = rs_slots[group]
        begin = STARTS[group]
        return gram[rows_own, begin : begin + WIDTH] + slots[0] + slots[1] + slots[2]

    def child_sums(name, own, slots, both):
        column_out[name].wait_recv()
        both[:, :RANK] = own[...] + slots[0]
        both[:, RANK:] = slots[1] + slots[2]
        gram_out[name].start()

    @pl.when(core == 0)
    def _():
        with jax.named_scope("gram_rows"):
            got = dealt(0, own_q)
            s43_own[...] = got[:, :RANK]
            s10_own[...] = got[:, RANK:]
            gram_out["43"].start()
            column_out["10"].start()
            got = dealt(2, own_q)
            s42_own[...] = got[:, :RANK]
            s32_own[...] = got[:, RANK:]
            column_out["32"].start()
            gram_out["42"].start()
            plane_own[...] = dealt(1, own_y)
            plane_out.start()
            got = dealt(3, own_q)
            s31_own[...] = got[:, :RANK]
            s30_own[...] = got[:, RANK:]
            column_out["31"].start()
            column_out["30"].start()
            got = dealt(4, own_q)
            s41_own[...] = got[:, :RANK]
            s40_own[...] = got[:, RANK:]
            gram_out["41"].start()
            gram_out["40"].start()
        with jax.named_scope("gram_plane10"):
            column_out["10"].wait_recv()
            t10_own[...] = s10_own[...] + s10_y[0] + s10_y[1] + s10_y[2]
            pair_out.start()
        with jax.named_scope("gram_children"):
            child_sums("32", s32_own, s32_y, t32_own)
            child_sums("31", s31_own, s31_y, t31_own)
        with jax.named_scope("gram_plane_sum"):
            plane_out.wait_recv()
            t2_own[...] = plane_own[...] + plane_x[0] + plane_x[1] + plane_x[2]
            gram_out["2"].start()
        with jax.named_scope("gram_children"):
            child_sums("30", s30_own, s30_y, t30_own)
        with jax.named_scope("gram_pair"):
            pair_out.wait_recv()
            u10_own[:, :RANK] = t10_own[...] + t10_z[0]
            u10_own[:, RANK:] = t10_z[1] + t10_z[2]
            gram_out["10"].start()
        with jax.named_scope("field_update"):
            z_wait(z_rest, 2, 5, 0)
            z_wait(z_one, 1, 2, 0)
            subtract((1, 2, 3, 4), field)
            z_wait(z_low, 0, 1, 0)
            subtract((0,), out)
        with jax.named_scope("sent"):
            for stage in (
                gram_rs
                + list(gram_out.values())
                + list(column_out.values())
                + [plane_out, pair_out]
                + proj_pair
            ):
                stage.wait_send()

    def child_side(level):
        return ((y % 2), (y // 2), (z % 2), (z // 2) % 2, (z // 4))[4 - level]

    def solve(level, own, sibling):
        side = child_side(level)
        first = jnp.where(side == 0, own, sibling)
        second = jnp.where(side == 0, sibling, own)
        high, low = two_parts(jnp.concatenate([first, second], 1))
        got = dot_nt(jnp.concatenate([high, low], 0), caps[level, 0])
        rounded = (got[:QUARTER] + got[QUARTER:]).astype(BF16)
        left, right = rounded[:, :RANK], rounded[:, RANK:]
        near = jnp.where(side == 0, left, right)
        far = jnp.where(side == 0, right, left)
        zown[level] = near.astype(F32)
        zbuf[level, own_q, :] = near.astype(F32)
        return near, far

    p4_out = Stage(
        "p4",
        [(p4.at[quarter(flips(x, j))], p4_rs.at[j - 1], device(dx=j)) for j in (2, 3, 1)]
        + [(p4.at[quarter(flips(x, j))], p4_rs.at[3 + j], device(dx=j, dy=1)) for j in (2, 3, 1, 0)],
        p4_rs,
    )
    p3_out, p2_out, p10_out = [
        Stage(name, [(src.at[quarter(flips(x, j))], slots.at[j - 1], device(dx=j)) for j in (2, 3, 1)], slots)
        for name, src, slots in (("p3", p3, p3_rs), ("p2", p2, p2_rs), ("p10", p10, p10_rs))
    ]
    e3_out = Stage("e3", [(e3, l3.at[j - 1], device(dy=j)) for j in (1, 2, 3)], l3)
    e2_out = Stage("e2", [(e2, l2.at[j - 1], device(dy=j)) for j in (1, 2, 3)], l2)
    h1_out = Stage("h1", [(h1, k1.at[j - 1], device(dy=j)) for j in (1, 2, 3)], k1)
    h0_out = Stage("h0", [(h0, k0.at[j - 1], device(dy=j)) for j in (1, 2, 3)], k0)
    d2_out = Stage("d2", [(d2, m2, device(dz=1))], m2)
    e1_out = Stage("e1", [(e1, l1.at[j - 1], device(dz=j)) for j in (3, 2, 1)], l1)
    f0_out = Stage("f0", [(f0, l1r.at[j - 1], device(dz=j)) for j in (3, 2, 1)], l1r)
    at_end = (z % 4) * (3 - z % 4) == 0
    inside = (z % 4) * (3 - z % 4) != 0

    def ends_first(stage):
        @pl.when(at_end)
        def _():
            stage.start(slice(0, 1))

        @pl.when(inside)
        def _():
            stage.start(slice(1, 3))

    def the_others(stages):
        @pl.when(at_end)
        def _():
            for stage in stages:
                stage.start(slice(1, 3))

        @pl.when(inside)
        def _():
            for stage in stages:
                stage.start(slice(0, 1))

    e0_out = Stage("e0", [(e0, l0, device(dz=j)) for j in (6, 7)], l0, e0_sent)

    @pl.when(core == 1)
    def _():
        with jax.named_scope("proj_pair"):
            for stage, ref, arrived, onward in zip(
                proj_pair, ordered, ordered_in, (p4_out, p3_out, p2_out, p10_out)
            ):
                stage.wait_recv()
                ref[...] += arrived[...]
                onward.start()

        with jax.named_scope("level4"):
            p4_out.wait_recv()
            own = p4[own_q, :] + p4_rs[0] + p4_rs[1] + p4_rs[2]
            z4, _ = solve(4, own, p4_rs[3] + p4_rs[4] + p4_rs[5] + p4_rs[6])
        with jax.named_scope("correct_by_4"):
            p3_out.wait_recv()
            gram_out["43"].wait_recv()
            own3 = p3[own_q, :] + p3_rs[0] + p3_rs[1] + p3_rs[2] - times_gram((z4, g43[...]))
            e3[...] = own3
            e3_out.start()
            p2_out.wait_recv()
            gram_out["42"].wait_recv()
            own2 = p2[own_q, :] + p2_rs[0] + p2_rs[1] + p2_rs[2] - times_gram((z4, g42[...]))
            e2[...] = own2
            e2_out.start()
            p10_out.wait_recv()
            own10 = p10[own_q, :] + p10_rs[0] + p10_rs[1] + p10_rs[2]
            gram_out["41"].wait_recv()
            own1 = own10[:, RANK:] - times_gram((z4, g41[...]))
            h1[...] = own1
            h1_out.start()
            gram_out["40"].wait_recv()
            own0 = own10[:, :RANK] - times_gram((z4, g40[...]))
            h0[...] = own0
            h0_out.start()
        with jax.named_scope("level3"):
            e3_out.wait_recv()
            z3, y3 = solve(3, own3 + l3[0], l3[1] + l3[2])
        with jax.named_scope("correct_by_3"):
            e2_out.wait_recv()
            plane2 = own2 + l2[0] + l2[1] + l2[2]
            gram_out["32"].wait_recv()
            plane2 = plane2 - times_gram((z3, g32[:, :RANK]), (y3, g32[:, RANK:]))
            d2[...] = plane2
            d2_out.start()
            h1_out.wait_recv()
            gram_out["31"].wait_recv()
            plane1 = own1 + k1[0] + k1[1] + k1[2] - times_gram(
                (z3, g31[:, :RANK]), (y3, g31[:, RANK:])
            )
        with jax.named_scope("level2"):
            d2_out.wait_recv()
            z2, _ = solve(2, plane2, m2[...])
            gram_out["2"].wait_recv()
            plane1 = plane1 - times_gram((z2, g2[:, :RANK]))
            e1[...] = plane1
            ends_first(e1_out)
        with jax.named_scope("correct_0"):
            h0_out.wait_recv()
            gram_out["30"].wait_recv()
            plane0 = own0 + k0[0] + k0[1] + k0[2] - times_gram(
                (z3, g30[:, :RANK]), (y3, g30[:, RANK:]), (z2, g2[:, RANK:])
            )
            f0[...] = plane0
            ends_first(f0_out)
            the_others((e1_out, f0_out))
            z_rest.start()
        with jax.named_scope("level1"):
            e1_out.wait_recv()
            z1, y1 = solve(1, plane1 + l1[0], l1[1] + l1[2])
        with jax.named_scope("correct_by_1"):
            f0_out.wait_recv()
            near0, far0 = plane0 + l1r[0], l1r[1] + l1r[2]
            gram_out["10"].wait_recv()
            half0 = near0 + far0 - times_gram((z1, g10[:, :RANK]), (y1, g10[:, RANK:]))
            e0[...] = half0

            @pl.when(at_end)
            def _():
                e0_out.start()

            z_one.start()
        with jax.named_scope("level0"):
            e0_out.wait_recv()
            solve(0, half0, l0[...])
            z_low.start()
        with jax.named_scope("field_update"):
            z_wait(z_rest, 2, 5, 1)
            z_wait(z_one, 1, 2, 1)
            subtract((1, 2, 3, 4), field)
            z_wait(z_low, 0, 1, 1)
            subtract((0,), out)
        with jax.named_scope("sent"):
            for stage in gram_pair + [
                p4_out, p3_out, p2_out, p10_out, e3_out, e2_out, h1_out, h0_out, d2_out, e1_out, f0_out,
            ] + [z_rest, z_one, z_low]:
                stage.wait_send()

            @pl.when(at_end)
            def _():
                e0_out.wait_send()

    assert counter[0] == STAGES


STAGES = 42


def vmem(*shape, dtype=F32):
    return pltpu.VMEM(shape, dtype)


def tree_solve(loads, inverse, bases, caps):
    rows = loads.shape[0]
    q = QUARTER
    scratch = [
        vmem(rows, CASES, dtype=BF16), vmem(rows, rows, dtype=BF16),
        vmem(rows, LEVELS * RANK, dtype=BF16), vmem(*caps.shape, dtype=BF16),
        vmem(rows, CASES),
    ]
    scratch += [vmem(RANK, WIDTH * len(GROUPS))] * 2
    scratch += [vmem(3, q, WIDTH)] * len(GROUPS)
    scratch += [vmem(q, RANK)] * 8 + [vmem(3, q, RANK)] * 4
    scratch += [vmem(q, WIDTH), vmem(3, q, WIDTH)] + [vmem(q, WIDTH)] * 4
    scratch += [vmem(q, RANK), vmem(3, q, RANK), vmem(q, WIDTH)]
    scratch += [vmem(RANK, width * RANK) for width in (1, 1, 2, 1, 2, 1, 2, 2, 2)]
    scratch += [vmem(CASES, width * RANK) for width in (1, 1, 1, 2)] * 2
    scratch += [vmem(7, q, RANK), vmem(3, q, RANK), vmem(3, q, RANK), vmem(3, q, 2 * RANK)]
    scratch += [vmem(q, RANK), vmem(3, q, RANK)] * 4
    scratch += [vmem(q, RANK), vmem(q, RANK)]
    scratch += [vmem(q, RANK), vmem(3, q, RANK)] * 2 + [vmem(q, RANK), vmem(q, RANK), vmem(2 * q, RANK)]
    scratch += [vmem(LEVELS, q, RANK), vmem(LEVELS, CASES, RANK), vmem(LEVELS, 7 * q, RANK)]
    scratch += [
        pltpu.SemaphoreType.DMA((LEVELS + 2,)),
        pltpu.SemaphoreType.DMA((3,)),
        pltpu.SemaphoreType.DMA,
        pltpu.SemaphoreType.DMA((STAGES,)),
    ]
    anywhere = pl.BlockSpec(memory_space=pl.ANY)
    return pl.pallas_call(
        tree_kernel,
        out_shape=pltpu.VMEM((rows, CASES), F32),
        in_specs=[anywhere] * 4,
        out_specs=pl.BlockSpec(memory_space=pltpu.VMEM),
        scratch_shapes=scratch,
        compiler_params=pltpu.CompilerParams(
            collective_id=0, has_side_effects=True, vmem_limit_bytes=60 * 2**20
        ),
        name="tree_solve",
    )(loads, inverse, bases, caps)


def local(loads, leaf_inverse, bases, couplings):
    return tree_solve(loads, leaf_inverse, bases, couplings)


def solution(mesh):
    in_specs = (
        P("leaf", None),
        P("leaf", None),
        P(None, "leaf", None),
        P(None, "leaf", None, None),
    )
    return jax.shard_map(
        local, mesh=mesh, in_specs=in_specs, out_specs=P("leaf", None), check_vma=False
    )
```

```python
import jax
import jax.numpy as jnp
from jax import lax
from jax.experimental import pallas as pl
from jax.experimental.pallas import tpu as pltpu
from jax.sharding import PartitionSpec as P

MESH = pl.DeviceIdType.MESH
F32 = jnp.float32
BF16 = jnp.bfloat16
RANK = 128
CASES = 128
LEVELS = 5
QUARTER = CASES // 4
ROWS = 512
TILE = 256


def flip(value, bit):
    return value + bit - 2 * bit * ((value // bit) % 2)


def flips(value, mask):
    for bit in (1, 2, 4):
        if mask & bit:
            value = flip(value, bit)
    return value


def dot_tn(a, b):
    return lax.dot_general(a, b, (((0,), (0,)), ((), ())), preferred_element_type=F32)


def dot_nt(a, b):
    return lax.dot_general(a, b, (((1,), (1,)), ((), ())), preferred_element_type=F32)


def two_parts(value):
    high = value.astype(BF16)
    return high, (value - high.astype(F32)).astype(BF16)


def times_gram(*pairs):
    rows, columns = [], []
    for z, gram in pairs:
        rows += [z, z]
        columns += two_parts(gram)
    return jnp.dot(
        jnp.concatenate(rows, 1), jnp.concatenate(columns, 0), preferred_element_type=F32
    )


GROUPS = (
    ((4, 3), (1, 0)),
    ((2, 1), (2, 0)),
    ((4, 2), (3, 2)),
    ((3, 1), (3, 0)),
    ((4, 1), (4, 0)),
)
WIDTH = 2 * RANK
STARTS = tuple(WIDTH * at for at in range(len(GROUPS)))
PIECES = ((0, 2 * WIDTH), (2 * WIDTH, 4 * WIDTH), (4 * WIDTH, 5 * WIDTH))


def tree_kernel(
    loads_hbm, inverse_hbm, bases_hbm, caps_hbm,
    out,
    loads, inverse, bcat, caps, field,
    gram, gram_in, s0_rs, s1_rs, s2_rs, s3_rs, s4_rs,
    s43_own, s10_own, s42_own, s32_own, s31_own, s30_own, s41_own, s40_own, s32_y, s31_y, s30_y, s10_y,
    plane_own, plane_x, t32_own, t31_own, t30_own, t2_own, t10_own, t10_z, u10_own,
    g43, g42, g32, g41, g31, g40, g30, g2, g10,
    p4, p3, p2, p10, p4_in, p3_in, p2_in, p10_in, p4_rs, p3_rs, p2_rs, p10_rs,
    e3, l3, e2, l2, h1, k1, h0, k0, d2, m2, e1, l1, f0, l1r, e0, l0, e0_sent,
    zown, zbuf, z_sent,
    local_sem, chunk_sem, send_sem, recv_sem,
):
    rows = field.shape[0]
    me = lax.axis_index("leaf")
    core = me % 2
    x = (me // 2) % 4
    y = (me // 8) % 4
    z = me // 32

    def device(dx=0, dy=0, dz=0, on=1):
        return ((flips(z, dz) * 4 + flips(y, dy)) * 4 + flips(x, dx)) * 2 + on

    loads_in = []
    for level in range(LEVELS):
        copy = pltpu.make_async_copy(
            bases_hbm.at[level], bcat.at[:, pl.ds(level * RANK, RANK)], local_sem.at[level]
        )
        copy.start()
        loads_in.append(copy)
    loads_copy = pltpu.make_async_copy(loads_hbm, loads, local_sem.at[LEVELS])
    loads_copy.start()
    caps_copy = pltpu.make_async_copy(caps_hbm, caps, local_sem.at[LEVELS + 1])

    chunks = ((0, rows // 4), (rows // 4, rows // 4), (rows // 2, rows // 2))

    def inverse_copy(step):
        part = pl.ds(*chunks[step])
        return pltpu.make_async_copy(inverse_hbm.at[part], inverse.at[part], chunk_sem.at[step])

    barrier = pltpu.get_barrier_semaphore()

    def greet(partners):
        for partner in partners:
            pl.semaphore_signal(barrier, inc=1, device_id=(partner,), device_id_type=MESH)

    gram_partners = (
        [device(dx=j, on=0) for j in (1, 2, 3)]
        + [device(dy=j, on=0) for j in (1, 2, 3)]
        + [device(dz=j, on=0) for j in (1, 2, 3)]
        + [device(dx=j, on=1) for j in range(4)]
        + [device(dy=j, on=1) for j in (1, 2, 3)]
    )
    chain_partners = (
        [device(dx=j, on=0) for j in range(4)]
        + [device(dy=j, on=0) for j in (1, 2, 3)]
        + [device(dx=j) for j in (1, 2, 3)]
        + [device(dx=j, dy=1) for j in range(4)]
        + [device(dy=j) for j in (2, 3)]
        + [device(dz=j) for j in (1, 2, 3, 6, 7)]
    )

    @pl.when(core == 0)
    def _():
        greet(gram_partners)

    @pl.when(core == 1)
    def _():
        greet(chain_partners)

    for step in range(len(chunks)):
        inverse_copy(step).start()
    caps_copy.start()

    with jax.named_scope("bases_in"):
        for copy in loads_in:
            copy.wait()
    with jax.named_scope("gram_blocks"):
        for level in (4, 3, 2, 1):
            got = dot_tn(bcat[:, level * RANK : (level + 1) * RANK], bcat[:, : level * RANK])
            for begin, group in zip(STARTS, GROUPS):
                for place, (source, target) in enumerate(group):
                    if source == level:
                        at = begin + place * RANK
                        gram[:, at : at + RANK] = got[:, target * RANK : (target + 1) * RANK]

    @pl.when(core == 0)
    def _():
        with jax.named_scope("meet"):
            pl.semaphore_wait(barrier, len(gram_partners))

    @pl.when(core == 1)
    def _():
        with jax.named_scope("meet"):
            pl.semaphore_wait(barrier, len(chain_partners))

    counter = {"both": 0, "core0": 3, "core1": 3}

    class Stage:
        def __init__(self, name, copies, arrive, leave=None, heard="core1"):
            self.name = name
            self.number = counter[heard]
            counter[heard] += 1
            self.copies = copies
            self.arrive = arrive
            self.leave = arrive if leave is None else leave

        def describe(self, src, dst, target):
            return pltpu.make_async_remote_copy(
                src_ref=src, dst_ref=dst,
                send_sem=send_sem, recv_sem=recv_sem.at[self.number],
                device_id=(target,), device_id_type=MESH,
            )

        def start(self, which=slice(None)):
            for copy in self.copies[which]:
                self.describe(*copy).start()

        def wait_recv(self, arrive=None):
            ref = self.arrive if arrive is None else arrive
            with jax.named_scope("wait_" + self.name):
                self.describe(ref, ref, self.copies[0][2]).wait_recv()

        def wait_send(self):
            self.describe(self.leave, self.leave, self.copies[0][2]).wait_send()

    def quarter(index):
        return pl.ds(pl.multiple_of(index * QUARTER, QUARTER), QUARTER)

    other = device(on=1 - core)
    gram_pair = [
        Stage("gram_in", [(gram.at[:, low:high], gram_in.at[:, low:high], other)], gram_in.at[:, low:high], heard="core0")
        for low, high in PIECES
    ]

    @pl.when(core == 1)
    def _():
        for stage in gram_pair:
            stage.start()

    loads_copy.wait()

    def field_step(step):
        with jax.named_scope("inverse_in"):
            inverse_copy(step).wait()
        with jax.named_scope("field"):
            begin, size = chunks[step]
            for at in range(begin, begin + size, TILE):
                part = pl.ds(at, TILE)
                field[part, :] = jnp.dot(inverse[part, :], loads[...], preferred_element_type=F32)

    field_step(0)

    rs_slots = (s0_rs, s1_rs, s2_rs, s3_rs, s4_rs)

    def deal(group):
        columns, slots = pl.ds(STARTS[group], WIDTH), rs_slots[group]
        if group == 1:
            copies = [
                (gram.at[quarter(flips(y, j)), columns], slots.at[j - 1], device(dy=j, on=0))
                for j in (2, 3, 1)
            ]
        else:
            copies = [
                (gram.at[quarter(flips(x, j)), columns], slots.at[j - 1], device(dx=j, on=0))
                for j in (2, 3, 1)
            ]
        return Stage("gram_row%d" % group, copies, slots, heard="core0")

    gram_rs = [deal(group) for group in range(len(GROUPS))]

    def pair_sum(piece):
        with jax.named_scope("pair_sums"):
            low, high = PIECES[piece]
            gram_pair[piece].wait_recv()
            gram[:, low:high] += gram_in[:, low:high]

    @pl.when(core == 0)
    def _():
        pair_sum(0)
        gram_rs[0].start()
        gram_rs[1].start()

    field_step(1)

    @pl.when(core == 0)
    def _():
        pair_sum(1)
        gram_rs[2].start()
        gram_rs[3].start()

    field_step(2)

    ordered = (p4, p3, p2, p10)
    with jax.named_scope("projections"):
        field_b = field[...].astype(BF16)
        got = dot_tn(field_b, bcat[:, 3 * RANK :])
        p4[...] = got[:, RANK:]
        p3[...] = got[:, :RANK]
    ordered_in = (p4_in, p3_in, p2_in, p10_in)
    proj_pair = [Stage("proj_in", [(src, dst, other)], dst) for src, dst in zip(ordered, ordered_in)]
    own_q = quarter(x)

    @pl.when(core == 0)
    def _():
        proj_pair[0].start()
        proj_pair[1].start()

    with jax.named_scope("projection_2"):
        p2[...] = dot_tn(field_b, bcat[:, 2 * RANK : 3 * RANK])

    @pl.when(core == 0)
    def _():
        proj_pair[2].start()
        pair_sum(2)
        gram_rs[4].start()

    with jax.named_scope("projections_10"):
        p10[...] = dot_tn(field_b, bcat[:, : 2 * RANK])

    @pl.when(core == 0)
    def _():
        proj_pair[3].start()

    z_targets = [(j, on) for on in (0, 1) for j in (2, 3, 1, 0) if (j, on) != (0, 1)]

    def z_stage(low, high):
        levels = pl.ds(low, high - low)
        return Stage(
            "z%d" % low,
            [
                (zown.at[levels], zbuf.at[levels, own_q], device(dx=j, on=on))
                for j, on in z_targets
            ],
            zbuf.at[levels], z_sent.at[levels], heard="both",
        )

    z_low, z_one, z_rest = z_stage(0, 1), z_stage(1, 2), z_stage(2, 5)

    def z_wait(stage, low, high, on):
        stage.wait_recv(zbuf.at[pl.ds(low, high - low), pl.ds(0, (4 - on) * QUARTER)])

    def subtract(levels, into):
        factors = jnp.concatenate([zbuf[level].astype(BF16) for level in levels], 1)
        low, high = levels[0] * RANK, (levels[-1] + 1) * RANK
        for begin in range(0, rows, ROWS):
            part = pl.ds(begin, ROWS)
            into[part, :] = field[part, :] - dot_nt(bcat[part, low:high], factors)

    caps_copy.wait()

    own_y = quarter(y)
    gram_out = {
        name: Stage("gram_" + name, [(src, dst.at[own_q], device(dx=j)) for j in (2, 3, 1, 0)], dst)
        for name, src, dst in (
            ("43", s43_own, g43), ("42", s42_own, g42), ("32", t32_own, g32), ("41", s41_own, g41),
            ("31", t31_own, g31), ("40", s40_own, g40), ("30", t30_own, g30), ("10", u10_own, g10),
        )
    }
    gram_out["2"] = Stage("gram_2", [(t2_own, g2.at[own_y], device(dy=j)) for j in (2, 3, 1, 0)], g2)
    column_out = {
        name: Stage(
            "column" + name, [(src, dst.at[j - 1], device(dy=j, on=0)) for j in (2, 3, 1)], dst, heard="core0"
        )
        for name, src, dst in (
            ("32", s32_own, s32_y), ("31", s31_own, s31_y), ("30", s30_own, s30_y), ("10", s10_own, s10_y),
        )
    }
    plane_out = Stage(
        "plane", [(plane_own, plane_x.at[j - 1], device(dx=j, on=0)) for j in (2, 3, 1)], plane_x, heard="core0"
    )
    pair_out = Stage("pair", [(t10_own, t10_z.at[j - 1], device(dz=j, on=0)) for j in (3, 2, 1)], t10_z, heard="core0")

    def dealt(group, rows_own):
        gram_rs[group].wait_recv()
        slots = rs_slots[group]
        begin = STARTS[group]
        return gram[rows_own, begin : begin + WIDTH] + slots[0] + slots[1] + slots[2]

    def child_sums(name, own, slots, both):
        column_out[name].wait_recv()
        both[:, :RANK] = own[...] + slots[0]
        both[:, RANK:] = slots[1] + slots[2]
        gram_out[name].start()

    @pl.when(core == 0)
    def _():
        with jax.named_scope("gram_rows"):
            got = dealt(0, own_q)
            s43_own[...] = got[:, :RANK]
            s10_own[...] = got[:, RANK:]
            gram_out["43"].start()
            column_out["10"].start()
            got = dealt(2, own_q)
            s42_own[...] = got[:, :RANK]
            s32_own[...] = got[:, RANK:]
            column_out["32"].start()
            gram_out["42"].start()
            plane_own[...] = dealt(1, own_y)
            plane_out.start()
            got = dealt(3, own_q)
            s31_own[...] = got[:, :RANK]
            s30_own[...] = got[:, RANK:]
            column_out["31"].start()
            column_out["30"].start()
            got = dealt(4, own_q)
            s41_own[...] = got[:, :RANK]
            s40_own[...] = got[:, RANK:]
            gram_out["41"].start()
            gram_out["40"].start()
        with jax.named_scope("gram_plane10"):
            column_out["10"].wait_recv()
            t10_own[...] = s10_own[...] + s10_y[0] + s10_y[1] + s10_y[2]
            pair_out.start()
        with jax.named_scope("gram_children"):
            child_sums("32", s32_own, s32_y, t32_own)
            child_sums("31", s31_own, s31_y, t31_own)
        with jax.named_scope("gram_plane_sum"):
            plane_out.wait_recv()
            t2_own[...] = plane_own[...] + plane_x[0] + plane_x[1] + plane_x[2]
            gram_out["2"].start()
        with jax.named_scope("gram_children"):
            child_sums("30", s30_own, s30_y, t30_own)
        with jax.named_scope("gram_pair"):
            pair_out.wait_recv()
            u10_own[:, :RANK] = t10_own[...] + t10_z[0]
            u10_own[:, RANK:] = t10_z[1] + t10_z[2]
            gram_out["10"].start()
        with jax.named_scope("field_update"):
            z_wait(z_rest, 2, 5, 0)
            z_wait(z_one, 1, 2, 0)
            subtract((1, 2, 3, 4), field)
            z_wait(z_low, 0, 1, 0)
            subtract((0,), out)
        with jax.named_scope("sent"):
            for stage in (
                gram_rs
                + list(gram_out.values())
                + list(column_out.values())
                + [plane_out, pair_out]
                + proj_pair
            ):
                stage.wait_send()

    def child_side(level):
        return ((y % 2), (y // 2), (z % 2), (z // 2) % 2, (z // 4))[4 - level]

    def solve(level, own, sibling):
        side = child_side(level)
        first = jnp.where(side == 0, own, sibling)
        second = jnp.where(side == 0, sibling, own)
        high, low = two_parts(jnp.concatenate([first, second], 1))
        got = dot_nt(jnp.concatenate([high, low], 0), caps[level, 0])
        rounded = (got[:QUARTER] + got[QUARTER:]).astype(BF16)
        left, right = rounded[:, :RANK], rounded[:, RANK:]
        near = jnp.where(side == 0, left, right)
        far = jnp.where(side == 0, right, left)
        zown[level] = near.astype(F32)
        zbuf[level, own_q, :] = near.astype(F32)
        return near, far

    p4_out = Stage(
        "p4",
        [(p4.at[quarter(flips(x, j))], p4_rs.at[j - 1], device(dx=j)) for j in (2, 3, 1)]
        + [(p4.at[quarter(flips(x, j))], p4_rs.at[3 + j], device(dx=j, dy=1)) for j in (2, 3, 1, 0)],
        p4_rs,
    )
    p3_out, p2_out, p10_out = [
        Stage(name, [(src.at[quarter(flips(x, j))], slots.at[j - 1], device(dx=j)) for j in (2, 3, 1)], slots)
        for name, src, slots in (("p3", p3, p3_rs), ("p2", p2, p2_rs), ("p10", p10, p10_rs))
    ]
    e3_out = Stage("e3", [(e3, l3.at[j - 1], device(dy=j)) for j in (1, 2, 3)], l3)
    e2_out = Stage("e2", [(e2, l2.at[j - 1], device(dy=j)) for j in (1, 2, 3)], l2)
    h1_out = Stage("h1", [(h1, k1.at[j - 1], device(dy=j)) for j in (1, 2, 3)], k1)
    h0_out = Stage("h0", [(h0, k0.at[j - 1], device(dy=j)) for j in (1, 2, 3)], k0)
    d2_out = Stage("d2", [(d2, m2, device(dz=1))], m2)
    e1_out = Stage("e1", [(e1, l1.at[j - 1], device(dz=j)) for j in (3, 2, 1)], l1)
    f0_out = Stage("f0", [(f0, l1r.at[j - 1], device(dz=j)) for j in (3, 2, 1)], l1r)
    at_end = (z % 4) * (3 - z % 4) == 0
    inside = (z % 4) * (3 - z % 4) != 0

    def ends_first(stage):
        @pl.when(at_end)
        def _():
            stage.start(slice(0, 1))

        @pl.when(inside)
        def _():
            stage.start(slice(1, 3))

    def the_others(stages):
        @pl.when(at_end)
        def _():
            for stage in stages:
                stage.start(slice(1, 3))

        @pl.when(inside)
        def _():
            for stage in stages:
                stage.start(slice(0, 1))

    e0_out = Stage("e0", [(e0, l0, device(dz=j)) for j in (6, 7)], l0, e0_sent)

    @pl.when(core == 1)
    def _():
        with jax.named_scope("proj_pair"):
            for stage, ref, arrived, onward in zip(
                proj_pair, ordered, ordered_in, (p4_out, p3_out, p2_out, p10_out)
            ):
                stage.wait_recv()
                ref[...] += arrived[...]
                onward.start()

        with jax.named_scope("level4"):
            p4_out.wait_recv()
            own = p4[own_q, :] + p4_rs[0] + p4_rs[1] + p4_rs[2]
            z4, _ = solve(4, own, p4_rs[3] + p4_rs[4] + p4_rs[5] + p4_rs[6])
        with jax.named_scope("correct_by_4"):
            p3_out.wait_recv()
            gram_out["43"].wait_recv()
            own3 = p3[own_q, :] + p3_rs[0] + p3_rs[1] + p3_rs[2] - times_gram((z4, g43[...]))
            e3[...] = own3
            e3_out.start()
            p2_out.wait_recv()
            gram_out["42"].wait_recv()
            own2 = p2[own_q, :] + p2_rs[0] + p2_rs[1] + p2_rs[2] - times_gram((z4, g42[...]))
            e2[...] = own2
            e2_out.start()
            p10_out.wait_recv()
            own10 = p10[own_q, :] + p10_rs[0] + p10_rs[1] + p10_rs[2]
            gram_out["41"].wait_recv()
            own1 = own10[:, RANK:] - times_gram((z4, g41[...]))
            h1[...] = own1
            h1_out.start()
            gram_out["40"].wait_recv()
            own0 = own10[:, :RANK] - times_gram((z4, g40[...]))
            h0[...] = own0
            h0_out.start()
        with jax.named_scope("level3"):
            e3_out.wait_recv()
            z3, y3 = solve(3, own3 + l3[0], l3[1] + l3[2])
        with jax.named_scope("correct_by_3"):
            e2_out.wait_recv()
            plane2 = own2 + l2[0] + l2[1] + l2[2]
            gram_out["32"].wait_recv()
            plane2 = plane2 - times_gram((z3, g32[:, :RANK]), (y3, g32[:, RANK:]))
            d2[...] = plane2
            d2_out.start()
            h1_out.wait_recv()
            gram_out["31"].wait_recv()
            plane1 = own1 + k1[0] + k1[1] + k1[2] - times_gram(
                (z3, g31[:, :RANK]), (y3, g31[:, RANK:])
            )
        with jax.named_scope("level2"):
            d2_out.wait_recv()
            z2, _ = solve(2, plane2, m2[...])
            gram_out["2"].wait_recv()
            plane1 = plane1 - times_gram((z2, g2[:, :RANK]))
            e1[...] = plane1
            ends_first(e1_out)
        with jax.named_scope("correct_0"):
            h0_out.wait_recv()
            gram_out["30"].wait_recv()
            plane0 = own0 + k0[0] + k0[1] + k0[2] - times_gram(
                (z3, g30[:, :RANK]), (y3, g30[:, RANK:]), (z2, g2[:, RANK:])
            )
            f0[...] = plane0
            ends_first(f0_out)
            the_others((e1_out, f0_out))
            z_rest.start()
        with jax.named_scope("level1"):
            e1_out.wait_recv()
            z1, y1 = solve(1, plane1 + l1[0], l1[1] + l1[2])
        with jax.named_scope("correct_by_1"):
            f0_out.wait_recv()
            near0, far0 = plane0 + l1r[0], l1r[1] + l1r[2]
            gram_out["10"].wait_recv()
            half0 = near0 + far0 - times_gram((z1, g10[:, :RANK]), (y1, g10[:, RANK:]))
            e0[...] = half0

            @pl.when(at_end)
            def _():
                e0_out.start()

            z_one.start()
        with jax.named_scope("level0"):
            e0_out.wait_recv()
            solve(0, half0, l0[...])
            z_low.start()
        with jax.named_scope("field_update"):
            z_wait(z_rest, 2, 5, 1)
            z_wait(z_one, 1, 2, 1)
            subtract((1, 2, 3, 4), field)
            z_wait(z_low, 0, 1, 1)
            subtract((0,), out)
        with jax.named_scope("sent"):
            for stage in gram_pair + [
                p4_out, p3_out, p2_out, p10_out, e3_out, e2_out, h1_out, h0_out, d2_out, e1_out, f0_out,
            ] + [z_rest, z_one, z_low]:
                stage.wait_send()

            @pl.when(at_end)
            def _():
                e0_out.wait_send()

    assert max(counter.values()) == STAGES and counter["both"] == 3


STAGES = 28


def vmem(*shape, dtype=F32):
    return pltpu.VMEM(shape, dtype)


def tree_solve(loads, inverse, bases, caps):
    rows = loads.shape[0]
    q = QUARTER
    scratch = [
        vmem(rows, CASES, dtype=BF16), vmem(rows, rows, dtype=BF16),
        vmem(rows, LEVELS * RANK, dtype=BF16), vmem(*caps.shape, dtype=BF16),
        vmem(rows, CASES),
    ]
    scratch += [vmem(RANK, WIDTH * len(GROUPS))] * 2
    scratch += [vmem(3, q, WIDTH)] * len(GROUPS)
    scratch += [vmem(q, RANK)] * 8 + [vmem(3, q, RANK)] * 4
    scratch += [vmem(q, WIDTH), vmem(3, q, WIDTH)] + [vmem(q, WIDTH)] * 4
    scratch += [vmem(q, RANK), vmem(3, q, RANK), vmem(q, WIDTH)]
    scratch += [vmem(RANK, width * RANK) for width in (1, 1, 2, 1, 2, 1, 2, 2, 2)]
    scratch += [vmem(CASES, width * RANK) for width in (1, 1, 1, 2)] * 2
    scratch += [vmem(7, q, RANK), vmem(3, q, RANK), vmem(3, q, RANK), vmem(3, q, 2 * RANK)]
    scratch += [vmem(q, RANK), vmem(3, q, RANK)] * 4
    scratch += [vmem(q, RANK), vmem(q, RANK)]
    scratch += [vmem(q, RANK), vmem(3, q, RANK)] * 2 + [vmem(q, RANK), vmem(q, RANK), vmem(2 * q, RANK)]
    scratch += [vmem(LEVELS, q, RANK), vmem(LEVELS, CASES, RANK), vmem(LEVELS, 7 * q, RANK)]
    scratch += [
        pltpu.SemaphoreType.DMA((LEVELS + 2,)),
        pltpu.SemaphoreType.DMA((3,)),
        pltpu.SemaphoreType.DMA,
        pltpu.SemaphoreType.DMA((STAGES,)),
    ]
    anywhere = pl.BlockSpec(memory_space=pl.ANY)
    return pl.pallas_call(
        tree_kernel,
        out_shape=pltpu.VMEM((rows, CASES), F32),
        in_specs=[anywhere] * 4,
        out_specs=pl.BlockSpec(memory_space=pltpu.VMEM),
        scratch_shapes=scratch,
        compiler_params=pltpu.CompilerParams(
            collective_id=0, has_side_effects=True, vmem_limit_bytes=60 * 2**20
        ),
        name="tree_solve",
    )(loads, inverse, bases, caps)


def local(loads, leaf_inverse, bases, couplings):
    return tree_solve(loads, leaf_inverse, bases, couplings)


def solution(mesh):
    in_specs = (
        P("leaf", None),
        P("leaf", None),
        P(None, "leaf", None),
        P(None, "leaf", None, None),
    )
    return jax.shard_map(
        local, mesh=mesh, in_specs=in_specs, out_specs=P("leaf", None), check_vma=False
    )
```

```python
import jax
import jax.numpy as jnp
from jax import lax
from jax.experimental import pallas as pl
from jax.experimental.pallas import tpu as pltpu
from jax.sharding import PartitionSpec as P

MESH = pl.DeviceIdType.MESH
F32 = jnp.float32
BF16 = jnp.bfloat16
RANK = 128
CASES = 128
LEVELS = 5
QUARTER = CASES // 4
ROWS = 512
TILE = 256


def flip(value, bit):
    return value + bit - 2 * bit * ((value // bit) % 2)


def flips(value, mask):
    for bit in (1, 2, 4):
        if mask & bit:
            value = flip(value, bit)
    return value


def dot_tn(a, b):
    return lax.dot_general(a, b, (((0,), (0,)), ((), ())), preferred_element_type=F32)


def dot_nt(a, b):
    return lax.dot_general(a, b, (((1,), (1,)), ((), ())), preferred_element_type=F32)


def two_parts(value):
    high = value.astype(BF16)
    return high, (value - high.astype(F32)).astype(BF16)


def times_gram(*pairs):
    rows, columns = [], []
    for z, gram in pairs:
        rows += [z, z]
        columns += two_parts(gram)
    return jnp.dot(
        jnp.concatenate(rows, 1), jnp.concatenate(columns, 0), preferred_element_type=F32
    )


GROUPS = (
    ((4, 3), (1, 0)),
    ((2, 1), (2, 0)),
    ((4, 2), (3, 2)),
    ((3, 1), (3, 0)),
    ((4, 1), (4, 0)),
)
WIDTH = 2 * RANK
STARTS = tuple(WIDTH * at for at in range(len(GROUPS)))
PIECES = ((0, 2 * WIDTH), (2 * WIDTH, 4 * WIDTH), (4 * WIDTH, 5 * WIDTH))


def tree_kernel(
    loads_hbm, inverse_hbm, bases_hbm, caps_hbm,
    out,
    loads, inverse, bcat, caps, field,
    gram, gram_in, s0_rs, s1_rs, s2_rs, s3_rs, s4_rs,
    s43_own, s10_own, s42_own, s32_own, s31_own, s30_own, s41_own, s40_own, s32_y, s31_y, s30_y, s10_y,
    plane_own, plane_x, t32_own, t31_own, t30_own, t2_own, t10_own, t10_z, u10_own,
    g43, g42, g32, g41, g31, g40, g30, g2, g10,
    p4, p3, p2, p10, p4_in, p3_in, p2_in, p10_in, p4_rs, p3_rs, p2_rs, p10_rs,
    e3, l3, e2, l2, h1, k1, h0, k0, d2, m2, e1, l1, f0, l1r, e0, l0, e0_sent,
    zown, zbuf, z_sent,
    local_sem, chunk_sem, send_sem, recv_sem,
):
    rows = field.shape[0]
    me = lax.axis_index("leaf")
    core = me % 2
    x = (me // 2) % 4
    y = (me // 8) % 4
    z = me // 32

    def device(dx=0, dy=0, dz=0, on=1):
        return ((flips(z, dz) * 4 + flips(y, dy)) * 4 + flips(x, dx)) * 2 + on

    loads_in = []
    for level in range(LEVELS):
        copy = pltpu.make_async_copy(
            bases_hbm.at[level], bcat.at[:, pl.ds(level * RANK, RANK)], local_sem.at[level]
        )
        copy.start()
        loads_in.append(copy)
    loads_copy = pltpu.make_async_copy(loads_hbm, loads, local_sem.at[LEVELS])
    loads_copy.start()
    caps_copy = pltpu.make_async_copy(caps_hbm, caps, local_sem.at[LEVELS + 1])

    chunks = ((0, rows // 4), (rows // 4, rows // 4), (rows // 2, rows // 2))

    def inverse_copy(step):
        part = pl.ds(*chunks[step])
        return pltpu.make_async_copy(inverse_hbm.at[part], inverse.at[part], chunk_sem.at[step])

    barrier = pltpu.get_barrier_semaphore()

    def greet(partners):
        for partner in partners:
            pl.semaphore_signal(barrier, inc=1, device_id=(partner,), device_id_type=MESH)

    gram_partners = (
        [device(dx=j, on=0) for j in (1, 2, 3)]
        + [device(dy=j, on=0) for j in (1, 2, 3)]
        + [device(dz=j, on=0) for j in (1, 2, 3)]
        + [device(dx=j, on=1) for j in range(4)]
        + [device(dy=j, on=1) for j in (1, 2, 3)]
    )
    chain_partners = (
        [device(dx=j, on=0) for j in range(4)]
        + [device(dy=j, on=0) for j in (1, 2, 3)]
        + [device(dx=j) for j in (1, 2, 3)]
        + [device(dx=j, dy=1) for j in range(4)]
        + [device(dy=j) for j in (2, 3)]
        + [device(dz=j) for j in (1, 2, 3, 6, 7)]
    )

    @pl.when(core == 0)
    def _():
        greet(gram_partners)

    @pl.when(core == 1)
    def _():
        greet(chain_partners)

    for step in range(len(chunks)):
        inverse_copy(step).start()
    caps_copy.start()

    with jax.named_scope("bases_in"):
        for copy in loads_in:
            copy.wait()
    with jax.named_scope("gram_blocks"):
        for level in (4, 3, 2, 1):
            got = dot_tn(bcat[:, level * RANK : (level + 1) * RANK], bcat[:, : level * RANK])
            for begin, group in zip(STARTS, GROUPS):
                for place, (source, target) in enumerate(group):
                    if source == level:
                        at = begin + place * RANK
                        gram[:, at : at + RANK] = got[:, target * RANK : (target + 1) * RANK]

    @pl.when(core == 0)
    def _():
        with jax.named_scope("meet"):
            pl.semaphore_wait(barrier, len(gram_partners))

    @pl.when(core == 1)
    def _():
        with jax.named_scope("meet"):
            pl.semaphore_wait(barrier, len(chain_partners))

    counter = {"both": 0, "core0": 3, "core1": 3}

    class Stage:
        def __init__(self, name, copies, arrive, leave=None, heard="core1"):
            self.name = name
            self.number = counter[heard]
            counter[heard] += 1
            self.copies = copies
            self.arrive = arrive
            self.leave = arrive if leave is None else leave

        def describe(self, src, dst, target):
            return pltpu.make_async_remote_copy(
                src_ref=src, dst_ref=dst,
                send_sem=send_sem, recv_sem=recv_sem.at[self.number],
                device_id=(target,), device_id_type=MESH,
            )

        def start(self, which=slice(None)):
            for copy in self.copies[which]:
                self.describe(*copy).start()

        def wait_recv(self, arrive=None):
            ref = self.arrive if arrive is None else arrive
            with jax.named_scope("wait_" + self.name):
                self.describe(ref, ref, self.copies[0][2]).wait_recv()

        def wait_send(self):
            self.describe(self.leave, self.leave, self.copies[0][2]).wait_send()

    def quarter(index):
        return pl.ds(pl.multiple_of(index * QUARTER, QUARTER), QUARTER)

    other = device(on=1 - core)
    gram_pair = [
        Stage("gram_in", [(gram.at[:, low:high], gram_in.at[:, low:high], other)], gram_in.at[:, low:high], heard="core0")
        for low, high in PIECES
    ]

    @pl.when(core == 1)
    def _():
        for stage in gram_pair:
            stage.start()

    loads_copy.wait()

    def field_step(step):
        with jax.named_scope("inverse_in"):
            inverse_copy(step).wait()
        with jax.named_scope("field"):
            begin, size = chunks[step]
            for at in range(begin, begin + size, TILE):
                part = pl.ds(at, TILE)
                field[part, :] = jnp.dot(inverse[part, :], loads[...], preferred_element_type=F32)

    field_step(0)

    rs_slots = (s0_rs, s1_rs, s2_rs, s3_rs, s4_rs)

    def deal(group):
        columns, slots = pl.ds(STARTS[group], WIDTH), rs_slots[group]
        if group == 1:
            copies = [
                (gram.at[quarter(flips(y, j)), columns], slots.at[j - 1], device(dy=j, on=0))
                for j in (2, 3, 1)
            ]
        else:
            copies = [
                (gram.at[quarter(flips(x, j)), columns], slots.at[j - 1], device(dx=j, on=0))
                for j in (2, 3, 1)
            ]
        return Stage("gram_row%d" % group, copies, slots, heard="core0")

    gram_rs = [deal(group) for group in range(len(GROUPS))]

    def pair_sum(piece):
        with jax.named_scope("pair_sums"):
            low, high = PIECES[piece]
            gram_pair[piece].wait_recv()
            gram[:, low:high] += gram_in[:, low:high]

    @pl.when(core == 0)
    def _():
        pair_sum(0)
        gram_rs[0].start()
        gram_rs[1].start()

    field_step(1)

    @pl.when(core == 0)
    def _():
        pair_sum(1)
        gram_rs[2].start()
        gram_rs[3].start()

    field_step(2)

    ordered = (p4, p3, p2, p10)
    with jax.named_scope("projections"):
        field_b = field[...].astype(BF16)
        got = dot_tn(field_b, bcat[:, 2 * RANK :])
        p4[...] = got[:, 2 * RANK :]
        p3[...] = got[:, RANK : 2 * RANK]
        p2[...] = got[:, :RANK]
    ordered_in = (p4_in, p3_in, p2_in, p10_in)
    proj_pair = [Stage("proj_in", [(src, dst, other)], dst) for src, dst in zip(ordered, ordered_in)]
    own_q = quarter(x)

    @pl.when(core == 0)
    def _():
        proj_pair[0].start()
        proj_pair[1].start()

    @pl.when(core == 0)
    def _():
        proj_pair[2].start()
        pair_sum(2)
        gram_rs[4].start()

    with jax.named_scope("projections_10"):
        p10[...] = dot_tn(field_b, bcat[:, : 2 * RANK])

    @pl.when(core == 0)
    def _():
        proj_pair[3].start()

    z_targets = [(j, on) for on in (0, 1) for j in (2, 3, 1, 0) if (j, on) != (0, 1)]

    def z_stage(low, high):
        levels = pl.ds(low, high - low)
        return Stage(
            "z%d" % low,
            [
                (zown.at[levels], zbuf.at[levels, own_q], device(dx=j, on=on))
                for j, on in z_targets
            ],
            zbuf.at[levels], z_sent.at[levels], heard="both",
        )

    z_low, z_one, z_rest = z_stage(0, 1), z_stage(1, 2), z_stage(2, 5)

    def z_wait(stage, low, high, on):
        stage.wait_recv(zbuf.at[pl.ds(low, high - low), pl.ds(0, (4 - on) * QUARTER)])

    def subtract(levels, into):
        factors = jnp.concatenate([zbuf[level].astype(BF16) for level in levels], 1)
        low, high = levels[0] * RANK, (levels[-1] + 1) * RANK
        for begin in range(0, rows, ROWS):
            part = pl.ds(begin, ROWS)
            into[part, :] = field[part, :] - dot_nt(bcat[part, low:high], factors)

    caps_copy.wait()

    own_y = quarter(y)
    gram_out = {
        name: Stage("gram_" + name, [(src, dst.at[own_q], device(dx=j)) for j in (2, 3, 1, 0)], dst)
        for name, src, dst in (
            ("43", s43_own, g43), ("42", s42_own, g42), ("32", t32_own, g32), ("41", s41_own, g41),
            ("31", t31_own, g31), ("40", s40_own, g40), ("30", t30_own, g30), ("10", u10_own, g10),
        )
    }
    gram_out["2"] = Stage("gram_2", [(t2_own, g2.at[own_y], device(dy=j)) for j in (2, 3, 1, 0)], g2)
    column_out = {
        name: Stage(
            "column" + name, [(src, dst.at[j - 1], device(dy=j, on=0)) for j in (2, 3, 1)], dst, heard="core0"
        )
        for name, src, dst in (
            ("32", s32_own, s32_y), ("31", s31_own, s31_y), ("30", s30_own, s30_y), ("10", s10_own, s10_y),
        )
    }
    plane_out = Stage(
        "plane", [(plane_own, plane_x.at[j - 1], device(dx=j, on=0)) for j in (2, 3, 1)], plane_x, heard="core0"
    )
    pair_out = Stage("pair", [(t10_own, t10_z.at[j - 1], device(dz=j, on=0)) for j in (3, 2, 1)], t10_z, heard="core0")

    def dealt(group, rows_own):
        gram_rs[group].wait_recv()
        slots = rs_slots[group]
        begin = STARTS[group]
        return gram[rows_own, begin : begin + WIDTH] + slots[0] + slots[1] + slots[2]

    def child_sums(name, own, slots, both):
        column_out[name].wait_recv()
        both[:, :RANK] = own[...] + slots[0]
        both[:, RANK:] = slots[1] + slots[2]
        gram_out[name].start()

    @pl.when(core == 0)
    def _():
        with jax.named_scope("gram_rows"):
            got = dealt(0, own_q)
            s43_own[...] = got[:, :RANK]
            s10_own[...] = got[:, RANK:]
            gram_out["43"].start()
            column_out["10"].start()
            got = dealt(2, own_q)
            s42_own[...] = got[:, :RANK]
            s32_own[...] = got[:, RANK:]
            column_out["32"].start()
            gram_out["42"].start()
            plane_own[...] = dealt(1, own_y)
            plane_out.start()
            got = dealt(3, own_q)
            s31_own[...] = got[:, :RANK]
            s30_own[...] = got[:, RANK:]
            column_out["31"].start()
            column_out["30"].start()
            got = dealt(4, own_q)
            s41_own[...] = got[:, :RANK]
            s40_own[...] = got[:, RANK:]
            gram_out["41"].start()
            gram_out["40"].start()
        with jax.named_scope("gram_plane10"):
            column_out["10"].wait_recv()
            t10_own[...] = s10_own[...] + s10_y[0] + s10_y[1] + s10_y[2]
            pair_out.start()
        with jax.named_scope("gram_children"):
            child_sums("32", s32_own, s32_y, t32_own)
            child_sums("31", s31_own, s31_y, t31_own)
        with jax.named_scope("gram_plane_sum"):
            plane_out.wait_recv()
            t2_own[...] = plane_own[...] + plane_x[0] + plane_x[1] + plane_x[2]
            gram_out["2"].start()
        with jax.named_scope("gram_children"):
            child_sums("30", s30_own, s30_y, t30_own)
        with jax.named_scope("gram_pair"):
            pair_out.wait_recv()
            u10_own[:, :RANK] = t10_own[...] + t10_z[0]
            u10_own[:, RANK:] = t10_z[1] + t10_z[2]
            gram_out["10"].start()
        with jax.named_scope("field_update"):
            z_wait(z_rest, 2, 5, 0)
            z_wait(z_one, 1, 2, 0)
            subtract((1, 2, 3, 4), field)
            z_wait(z_low, 0, 1, 0)
            subtract((0,), out)
        with jax.named_scope("sent"):
            for stage in (
                gram_rs
                + list(gram_out.values())
                + list(column_out.values())
                + [plane_out, pair_out]
                + proj_pair
            ):
                stage.wait_send()

    def child_side(level):
        return ((y % 2), (y // 2), (z % 2), (z // 2) % 2, (z // 4))[4 - level]

    def solve(level, own, sibling):
        side = child_side(level)
        first = jnp.where(side == 0, own, sibling)
        second = jnp.where(side == 0, sibling, own)
        high, low = two_parts(jnp.concatenate([first, second], 1))
        got = dot_nt(jnp.concatenate([high, low], 0), caps[level, 0])
        rounded = (got[:QUARTER] + got[QUARTER:]).astype(BF16)
        left, right = rounded[:, :RANK], rounded[:, RANK:]
        near = jnp.where(side == 0, left, right)
        far = jnp.where(side == 0, right, left)
        zown[level] = near.astype(F32)
        zbuf[level, own_q, :] = near.astype(F32)
        return near, far

    p4_out = Stage(
        "p4",
        [(p4.at[quarter(flips(x, j))], p4_rs.at[j - 1], device(dx=j)) for j in (2, 3, 1)]
        + [(p4.at[quarter(flips(x, j))], p4_rs.at[3 + j], device(dx=j, dy=1)) for j in (2, 3, 1, 0)],
        p4_rs,
    )
    p3_out, p2_out, p10_out = [
        Stage(name, [(src.at[quarter(flips(x, j))], slots.at[j - 1], device(dx=j)) for j in (2, 3, 1)], slots)
        for name, src, slots in (("p3", p3, p3_rs), ("p2", p2, p2_rs), ("p10", p10, p10_rs))
    ]
    e3_out = Stage("e3", [(e3, l3.at[j - 1], device(dy=j)) for j in (1, 2, 3)], l3)
    e2_out = Stage("e2", [(e2, l2.at[j - 1], device(dy=j)) for j in (1, 2, 3)], l2)
    h1_out = Stage("h1", [(h1, k1.at[j - 1], device(dy=j)) for j in (1, 2, 3)], k1)
    h0_out = Stage("h0", [(h0, k0.at[j - 1], device(dy=j)) for j in (1, 2, 3)], k0)
    d2_out = Stage("d2", [(d2, m2, device(dz=1))], m2)
    e1_out = Stage("e1", [(e1, l1.at[j - 1], device(dz=j)) for j in (3, 2, 1)], l1)
    f0_out = Stage("f0", [(f0, l1r.at[j - 1], device(dz=j)) for j in (3, 2, 1)], l1r)
    at_end = (z % 4) * (3 - z % 4) == 0
    inside = (z % 4) * (3 - z % 4) != 0

    def ends_first(stage):
        @pl.when(at_end)
        def _():
            stage.start(slice(0, 1))

        @pl.when(inside)
        def _():
            stage.start(slice(1, 3))

    def the_others(stages):
        @pl.when(at_end)
        def _():
            for stage in stages:
                stage.start(slice(1, 3))

        @pl.when(inside)
        def _():
            for stage in stages:
                stage.start(slice(0, 1))

    e0_out = Stage("e0", [(e0, l0, device(dz=j)) for j in (6, 7)], l0, e0_sent)

    @pl.when(core == 1)
    def _():
        with jax.named_scope("proj_pair"):
            for stage, ref, arrived, onward in zip(
                proj_pair, ordered, ordered_in, (p4_out, p3_out, p2_out, p10_out)
            ):
                stage.wait_recv()
                ref[...] += arrived[...]
                onward.start()

        with jax.named_scope("level4"):
            p4_out.wait_recv()
            own = p4[own_q, :] + p4_rs[0] + p4_rs[1] + p4_rs[2]
            z4, _ = solve(4, own, p4_rs[3] + p4_rs[4] + p4_rs[5] + p4_rs[6])
        with jax.named_scope("correct_by_4"):
            p3_out.wait_recv()
            gram_out["43"].wait_recv()
            own3 = p3[own_q, :] + p3_rs[0] + p3_rs[1] + p3_rs[2] - times_gram((z4, g43[...]))
            e3[...] = own3
            e3_out.start()
            p2_out.wait_recv()
            gram_out["42"].wait_recv()
            own2 = p2[own_q, :] + p2_rs[0] + p2_rs[1] + p2_rs[2] - times_gram((z4, g42[...]))
            e2[...] = own2
            e2_out.start()
            p10_out.wait_recv()
            own10 = p10[own_q, :] + p10_rs[0] + p10_rs[1] + p10_rs[2]
            gram_out["41"].wait_recv()
            own1 = own10[:, RANK:] - times_gram((z4, g41[...]))
            h1[...] = own1
            h1_out.start()
            gram_out["40"].wait_recv()
            own0 = own10[:, :RANK] - times_gram((z4, g40[...]))
            h0[...] = own0
            h0_out.start()
        with jax.named_scope("level3"):
            e3_out.wait_recv()
            z3, y3 = solve(3, own3 + l3[0], l3[1] + l3[2])
        with jax.named_scope("correct_by_3"):
            e2_out.wait_recv()
            plane2 = own2 + l2[0] + l2[1] + l2[2]
            gram_out["32"].wait_recv()
            plane2 = plane2 - times_gram((z3, g32[:, :RANK]), (y3, g32[:, RANK:]))
            d2[...] = plane2
            d2_out.start()
            h1_out.wait_recv()
            gram_out["31"].wait_recv()
            plane1 = own1 + k1[0] + k1[1] + k1[2] - times_gram(
                (z3, g31[:, :RANK]), (y3, g31[:, RANK:])
            )
        with jax.named_scope("level2"):
            d2_out.wait_recv()
            z2, _ = solve(2, plane2, m2[...])
            gram_out["2"].wait_recv()
            plane1 = plane1 - times_gram((z2, g2[:, :RANK]))
            e1[...] = plane1
            ends_first(e1_out)
        with jax.named_scope("correct_0"):
            h0_out.wait_recv()
            gram_out["30"].wait_recv()
            plane0 = own0 + k0[0] + k0[1] + k0[2] - times_gram(
                (z3, g30[:, :RANK]), (y3, g30[:, RANK:]), (z2, g2[:, RANK:])
            )
            f0[...] = plane0
            ends_first(f0_out)
            the_others((e1_out, f0_out))
            z_rest.start()
        with jax.named_scope("level1"):
            e1_out.wait_recv()
            z1, y1 = solve(1, plane1 + l1[0], l1[1] + l1[2])
        with jax.named_scope("correct_by_1"):
            f0_out.wait_recv()
            near0, far0 = plane0 + l1r[0], l1r[1] + l1r[2]
            gram_out["10"].wait_recv()
            half0 = near0 + far0 - times_gram((z1, g10[:, :RANK]), (y1, g10[:, RANK:]))
            e0[...] = half0

            @pl.when(at_end)
            def _():
                e0_out.start()

            z_one.start()
        with jax.named_scope("level0"):
            e0_out.wait_recv()
            solve(0, half0, l0[...])
            z_low.start()
        with jax.named_scope("field_update"):
            z_wait(z_rest, 2, 5, 1)
            z_wait(z_one, 1, 2, 1)
            subtract((1, 2, 3, 4), field)
            z_wait(z_low, 0, 1, 1)
            subtract((0,), out)
        with jax.named_scope("sent"):
            for stage in gram_pair + [
                p4_out, p3_out, p2_out, p10_out, e3_out, e2_out, h1_out, h0_out, d2_out, e1_out, f0_out,
            ] + [z_rest, z_one, z_low]:
                stage.wait_send()

            @pl.when(at_end)
            def _():
                e0_out.wait_send()

    assert max(counter.values()) == STAGES and counter["both"] == 3


STAGES = 28


def vmem(*shape, dtype=F32):
    return pltpu.VMEM(shape, dtype)


def tree_solve(loads, inverse, bases, caps):
    rows = loads.shape[0]
    q = QUARTER
    scratch = [
        vmem(rows, CASES, dtype=BF16), vmem(rows, rows, dtype=BF16),
        vmem(rows, LEVELS * RANK, dtype=BF16), vmem(*caps.shape, dtype=BF16),
        vmem(rows, CASES),
    ]
    scratch += [vmem(RANK, WIDTH * len(GROUPS))] * 2
    scratch += [vmem(3, q, WIDTH)] * len(GROUPS)
    scratch += [vmem(q, RANK)] * 8 + [vmem(3, q, RANK)] * 4
    scratch += [vmem(q, WIDTH), vmem(3, q, WIDTH)] + [vmem(q, WIDTH)] * 4
    scratch += [vmem(q, RANK), vmem(3, q, RANK), vmem(q, WIDTH)]
    scratch += [vmem(RANK, width * RANK) for width in (1, 1, 2, 1, 2, 1, 2, 2, 2)]
    scratch += [vmem(CASES, width * RANK) for width in (1, 1, 1, 2)] * 2
    scratch += [vmem(7, q, RANK), vmem(3, q, RANK), vmem(3, q, RANK), vmem(3, q, 2 * RANK)]
    scratch += [vmem(q, RANK), vmem(3, q, RANK)] * 4
    scratch += [vmem(q, RANK), vmem(q, RANK)]
    scratch += [vmem(q, RANK), vmem(3, q, RANK)] * 2 + [vmem(q, RANK), vmem(q, RANK), vmem(2 * q, RANK)]
    scratch += [vmem(LEVELS, q, RANK), vmem(LEVELS, CASES, RANK), vmem(LEVELS, 7 * q, RANK)]
    scratch += [
        pltpu.SemaphoreType.DMA((LEVELS + 2,)),
        pltpu.SemaphoreType.DMA((3,)),
        pltpu.SemaphoreType.DMA,
        pltpu.SemaphoreType.DMA((STAGES,)),
    ]
    anywhere = pl.BlockSpec(memory_space=pl.ANY)
    return pl.pallas_call(
        tree_kernel,
        out_shape=pltpu.VMEM((rows, CASES), F32),
        in_specs=[anywhere] * 4,
        out_specs=pl.BlockSpec(memory_space=pltpu.VMEM),
        scratch_shapes=scratch,
        compiler_params=pltpu.CompilerParams(
            collective_id=0, has_side_effects=True, vmem_limit_bytes=60 * 2**20
        ),
        name="tree_solve",
    )(loads, inverse, bases, caps)


def local(loads, leaf_inverse, bases, couplings):
    return tree_solve(loads, leaf_inverse, bases, couplings)


def solution(mesh):
    in_specs = (
        P("leaf", None),
        P("leaf", None),
        P(None, "leaf", None),
        P(None, "leaf", None, None),
    )
    return jax.shard_map(
        local, mesh=mesh, in_specs=in_specs, out_specs=P("leaf", None), check_vma=False
    )
```
